32 devices in a mesh: grp: 2 (over y), seq: 4 (over z), wid: 2 (over x), rep: 2 (over core).
Axes of the slice: x: 2, y: 2, z: 4, core: 2. Of those that a mesh axis runs over, the one named last changes fastest.
Arguments:
- activations: bfloat16 [8192, 8192], P(('grp', 'seq'), ('wid', 'rep')), parts along dimension 0, may hold values from -6 to 6
- output_grads: bfloat16 [8192, 8192], P(('grp', 'seq'), ('wid', 'rep')), parts along dimension 0, may hold values from -6 to 6
- act_exponents: int32 [128, 64], P(('grp', 'seq'), ('wid', 'rep')), parts along dimension 0, may hold values from -2 to 2
- grad_exponents: int32 [128, 64], P(('grp', 'seq'), ('wid', 'rep')), parts along dimension 0, may hold values from -2 to 2
- input_blocks: bfloat16 [16, 128, 64], P(('wid', 'rep')), may hold values from -0.125 to 0.125
- input_index: int32 [16], P(('wid', 'rep')), may hold values from 0 to 63, as said below
- output_blocks: bfloat16 [16, 128, 64], P(('wid', 'rep')), may hold values from -0.125 to 0.125
- output_index: int32 [16], P(('wid', 'rep')), may hold values from 0 to 63, as said below
- fisher_inverse: float32 [4096, 4096], P('seq', 'wid'), may hold values from -1 to 7, as said below
Outputs:
- preconditioned: float32 [64, 2, 4096], P(('grp', 'wid'), 'rep', 'seq'), parts along dimension 0
The draws below stay inside these ranges and needn't reach their ends.
There are 2 independent parts, one for each index of `grp`. The reference program is written for one: setup_inputs(seed, part) draws one part's arguments, and reference() takes and returns one part's arrays. A program takes and returns all parts, laid end to end along the dimension named above; an argument that names none is the same for every part. Nothing has to cross between parts.
Inputs may be any that keep to these rules, and one draw needn't show every extreme that they name: `input_index`: Rising; exactly one index in each aligned run of 4 blocks; the first block and the last block are always named. `output_index`: Rising; exactly one index in each aligned run of 4 blocks; the first block and the last block are always named. `fisher_inverse`: Symmetric.
All inputs are finite; a program needn't handle non-finite values.
Results may differ from the reference program's by a relative error of at most 0.00045.
Values sent between devices are 32-bit elements; how exact they have to be, the bound alone decides.
No kernel may reach another device: no remote copies, remote signals or barrier semaphores. Data moves between devices by JAX's collectives and lax.ppermute only.
A program may use at most 64 MiB of HBM per device.

```python
import jax
import jax.numpy as jnp
from jax import lax

D = 8192
R = 64
BLK = 128
BGROUP = 4
LEN = 64
NBLK = 64
NSEL = 16
Q = 4096
SEQS = 64
TOKENS = 4096
N_REP = 2


def block_choice(key):
    offsets = jax.random.randint(key, (NSEL,), 0, BGROUP)
    offsets = offsets.at[0].set(0).at[NSEL - 1].set(BGROUP - 1)
    return (jnp.arange(NSEL) * BGROUP + offsets).astype(jnp.int32)


def draw_input_index(key, part):
    return block_choice(jax.random.fold_in(key, 3))


def draw_output_index(key, part):
    return block_choice(jax.random.fold_in(key, 7))


def draw_fisher_inverse(key, part):
    key_diag, key_off = jax.random.split(jax.random.fold_in(key, 11))
    diagonal = jnp.exp(jax.random.uniform(key_diag, (Q,), jnp.float32, 0.0, 1.3862944))
    noise = jax.random.normal(key_off, (Q, Q), jnp.float32) * (0.4 / Q ** 0.5)
    offdiag = (noise + noise.T) * 0.5 ** 0.5
    return (offdiag + jnp.diag(diagonal)).astype(jnp.float32)


def with_ends(values, key, low, largest):
    shape = values.shape
    spot = [jax.random.randint(jax.random.fold_in(key, axis), (), 0, shape[axis]) for axis in range(len(shape))]
    values = values.at[tuple(spot)].set(low)
    longest = shape.index(max(shape))
    spot[longest] = (spot[longest] + 1) % shape[longest]
    return values.at[tuple(spot)].set(largest)


def level_of(stream_key, shape, cuts, smallest, top_value):
    gain = 1.0
    for axis_at, blocks in cuts:
        draws = jax.random.uniform(jax.random.fold_in(jax.random.fold_in(stream_key, 6), axis_at), (blocks,), jnp.float32, smallest / len(cuts), top_value / len(cuts))
        gain = gain * jnp.repeat(jnp.exp(draws), shape[axis_at] // blocks).reshape((-1,) + (1,) * (len(shape) - 1 - axis_at))
    return gain


def bell_draw(key, extent, width, limit, pieces=(), kind=jnp.bfloat16):
    array = width * jax.random.normal(key, extent, jnp.float32)
    if pieces:
        array = array * level_of(key, extent, pieces, -0.22, 0.18)
    return jnp.clip(array, -limit, limit).astype(kind)


def setup_inputs(seed: int = 0, part: int = 0) -> dict:
    arg_keys = jax.random.split(jax.random.key(seed), 10)
    own_keys = jax.random.split(jax.random.fold_in(arg_keys[9], part), 10)
    activations = bell_draw(own_keys[0], (TOKENS, D), 1.0, 6.0, ((0, 4), (1, 4)))
    output_grads = bell_draw(own_keys[1], (TOKENS, D), 1.0, 6.0, ((0, 4), (1, 4)))
    act_exponents = with_ends(jax.random.randint(own_keys[2], (SEQS, NBLK), -2, 3), jax.random.fold_in(own_keys[2], 1), -2, 2).astype(jnp.int32)
    grad_exponents = with_ends(jax.random.randint(own_keys[3], (SEQS, NBLK), -2, 3), jax.random.fold_in(own_keys[3], 1), -2, 2).astype(jnp.int32)
    input_blocks = bell_draw(arg_keys[4], (NSEL, BLK, R), (NSEL * BLK) ** -0.5, 0.125, ((0, 4),))
    input_index = draw_input_index(jax.random.fold_in(arg_keys[9], 71), part)
    output_blocks = bell_draw(arg_keys[6], (NSEL, BLK, R), (NSEL * BLK) ** -0.5, 0.125, ((0, 4),))
    output_index = draw_output_index(jax.random.fold_in(arg_keys[9], 71), part)
    fisher_inverse = draw_fisher_inverse(jax.random.fold_in(arg_keys[9], 71), part)
    return dict(activations=activations, output_grads=output_grads, act_exponents=act_exponents, grad_exponents=grad_exponents, input_blocks=input_blocks, input_index=input_index, output_blocks=output_blocks, output_index=output_index, fisher_inverse=fisher_inverse)


def select_blocks(values, exponents, index):
    seq_count = values.shape[0] // LEN
    blocks = values.reshape(seq_count, LEN, NBLK, BLK)
    picked = jnp.take(blocks, index, axis=2)
    scaling = jnp.exp2(jnp.take(exponents, index, axis=1).astype(jnp.float32)).astype(jnp.bfloat16)
    return (picked * scaling[:, None, :, None]).reshape(values.shape[0], NSEL * BLK)


def reference(activations, output_grads, act_exponents, grad_exponents, input_blocks, input_index, output_blocks, output_index, fisher_inverse):
    act_proj = jnp.dot(select_blocks(activations, act_exponents, input_index), input_blocks.reshape(NSEL * BLK, R), preferred_element_type=jnp.float32)
    grad_proj = jnp.dot(select_blocks(output_grads, grad_exponents, output_index), output_blocks.reshape(NSEL * BLK, R), preferred_element_type=jnp.float32)
    outer = jnp.einsum("sti,stj->sij", grad_proj.reshape(SEQS, LEN, R), act_proj.reshape(SEQS, LEN, R), precision=lax.Precision.HIGHEST) / LEN
    flat = outer.reshape(SEQS, Q)
    result = lax.dot_general(flat, fisher_inverse, (((1,), (1,)), ((), ())), precision=lax.Precision.HIGHEST, preferred_element_type=jnp.float32)
    return result.reshape(SEQS // N_REP, N_REP, Q)
```

```python
import functools

import jax
import jax.numpy as jnp
from jax import lax
from jax.experimental import pallas as pl
from jax.experimental.pallas import tpu as pltpu
from jax.sharding import PartitionSpec as P

BLK = 128
LEN = 64
NT = (((1,), (1,)), ((), ()))
F32 = jnp.float32
BF16 = jnp.bfloat16
VMEM = pl.BlockSpec(memory_space=pltpu.VMEM)
SMEM = pl.BlockSpec(memory_space=pltpu.SMEM)
HBM = pl.BlockSpec(memory_space=pltpu.HBM)
PARAMS = pltpu.CompilerParams(vmem_limit_bytes=16 << 20)


def two_parts(x):
    high = x.astype(BF16)
    return high, (x - high.astype(F32)).astype(BF16)


def product(left, right, dims):
    left_high, left_low = two_parts(left)
    right_high, right_low = two_parts(right)
    dot = functools.partial(lax.dot_general, dimension_numbers=dims, preferred_element_type=F32)
    return dot(left_high, right_high) + (dot(left_high, right_low) + dot(left_low, right_high))


def project_kernel(
    other,
    act_index,
    grad_index,
    act_exponents,
    grad_exponents,
    act_blocks,
    grad_blocks,
    acts,
    grads,
    out,
    picked,
    sems,
):
    rep = lax.axis_index("rep")
    parity = 1 - rep if other else rep
    block_count = act_exponents.shape[1]
    chosen = act_index.shape[0]
    pairs = acts.shape[0]
    sides = ((act_index, act_exponents, act_blocks, acts), (grad_index, grad_exponents, grad_blocks, grads))
    locals_ = []
    copies = []
    for side, (index, _, _, values) in enumerate(sides):
        for block in range(chosen):
            local = lax.rem(index[block], block_count)
            columns = pl.ds(pl.multiple_of(local * BLK, BLK), BLK)
            copy = pltpu.make_async_copy(
                values.at[:, parity, :, columns], picked.at[side, block], sems.at[side, block]
            )
            copy.start()
            locals_.append(local)
            copies.append(copy)
    for side, (_, exponents, blocks, _) in enumerate(sides):
        scaled = []
        for block in range(chosen):
            copies[side * chosen + block].wait()
            rows = []
            for pair in range(pairs):
                exponent = exponents[2 * pair + parity, locals_[side * chosen + block]]
                scale = jnp.exp2(jnp.full((LEN, BLK), exponent, jnp.int32).astype(F32)).astype(BF16)
                rows.append(picked[side, block, pair] * scale)
            scaled.append(jnp.concatenate(rows, axis=0))
        weights = jnp.concatenate([blocks[block] for block in range(chosen)], axis=1)
        width = weights.shape[0]
        out[side * width : (side + 1) * width, :] = lax.dot_general(
            weights, jnp.concatenate(scaled, axis=1), NT, preferred_element_type=F32
        )


def project(other, indices, exponents, blocks, values):
    pairs, _, _, features = values[0].shape
    chosen, width, _ = blocks[0].shape
    tokens = pairs * LEN
    return pl.pallas_call(
        functools.partial(project_kernel, other),
        out_shape=jax.ShapeDtypeStruct((2 * width, tokens), F32),
        in_specs=[SMEM] * 4 + [VMEM] * 2 + [HBM] * 2,
        out_specs=VMEM,
        scratch_shapes=[
            pltpu.VMEM((2, chosen, pairs, LEN, BLK), BF16),
            pltpu.SemaphoreType.DMA((2, chosen)),
        ],
        cost_estimate=pl.CostEstimate(
            flops=4 * tokens * chosen * BLK * width,
            bytes_accessed=4 * tokens * chosen * BLK + 8 * tokens * width,
            transcendentals=0,
        ),
        compiler_params=PARAMS,
        name="project_other" if other else "project_own",
    )(*indices, *exponents, *blocks, *values)


def split_kernel(fisher, high, low, held, sems):
    pieces = held.shape[0]
    rows = fisher.shape[0] // pieces
    copies = [
        pltpu.make_async_copy(fisher.at[pl.ds(piece * rows, rows)], held.at[piece], sems.at[piece])
        for piece in range(pieces)
    ]
    for copy in copies:
        copy.start()
    for piece in range(pieces):
        copies[piece].wait()

        @pl.loop(0, rows // 16)
        def _(step):
            part_high, part_low = two_parts(held[piece, pl.ds(step * 16, 16), :])
            target = pl.ds(piece * rows + step * 16, 16)
            high[target, :] = part_high
            low[target, :] = part_low


def split_fisher(fisher):
    rows, columns = fisher.shape
    pieces = 8
    half = jax.ShapeDtypeStruct((rows, columns), BF16)
    return pl.pallas_call(
        split_kernel,
        out_shape=(half, half),
        in_specs=[pl.BlockSpec(memory_space=pl.ANY)],
        out_specs=(VMEM, VMEM),
        scratch_shapes=[
            pltpu.VMEM((pieces, rows // pieces, columns), F32),
            pltpu.SemaphoreType.DMA((pieces,)),
        ],
        cost_estimate=pl.CostEstimate(
            flops=2 * rows * columns, bytes_accessed=8 * rows * columns, transcendentals=0
        ),
        compiler_params=PARAMS,
        name="split_fisher",
    )(fisher)


def message_kernel(width, own, other, *messages):
    wid = lax.axis_index("wid")
    count = len(messages) + 1
    share = width // count
    acts = own[:width, :] + other[:width, :]
    for shift, message in enumerate(messages, 1):
        target = lax.rem(wid + shift, count)
        rows = pl.ds(pl.multiple_of(width + target * share, share), share)
        message[:width, :] = acts
        message[width:, :] = own[rows, :] + other[rows, :]


def make_messages(own, other, wid_count):
    width = own.shape[0] // 2
    shape = jax.ShapeDtypeStruct((width + width // wid_count, own.shape[1]), F32)
    return pl.pallas_call(
        functools.partial(message_kernel, width),
        out_shape=[shape] * (wid_count - 1),
        in_specs=[VMEM] * 2,
        out_specs=[VMEM] * (wid_count - 1),
        compiler_params=PARAMS,
        name="make_messages",
    )(own, other)


def outer_kernel(width, own, other, *rest):
    *messages, out, staged = rest
    wid = lax.axis_index("wid")
    share = width // (len(messages) + 1)
    rows = pl.ds(pl.multiple_of(width + wid * share, share), share)
    acts = own[:width, :] + other[:width, :]
    grads = own[rows, :] + other[rows, :]
    for message in messages:
        acts = acts + message[:width, :]
        grads = grads + message[width:, :]
    half = share // 2
    pairs = acts.shape[1] // BLK
    lane = lax.broadcasted_iota(jnp.int32, (half, BLK), 1)
    for pair in range(pairs):
        columns = slice(pair * BLK, (pair + 1) * BLK)
        staged[pair] = grads[:, columns]
        pieces = []
        for odd in range(2):
            part = staged[pair, pl.ds(odd, half, stride=2), :]
            pieces.append(jnp.where(lane < LEN, part, 0.0))
            pieces.append(jnp.where(lane < LEN, 0.0, part))
        left = jnp.concatenate(pieces, axis=0)
        result = product(left, acts[:, columns], NT) * (1.0 / LEN)
        both = jnp.concatenate([result[: 2 * half, :], result[2 * half :, :]], axis=1)
        out[pl.ds(2 * pair, half, stride=2 * pairs), :] = both[:half, :]
        out[pl.ds(2 * pair + 1, half, stride=2 * pairs), :] = both[half:, :]


def outer_products(own, other, messages):
    width = own.shape[0] // 2
    tokens = own.shape[1]
    share = width // (len(messages) + 1)
    sequences = tokens // LEN
    return pl.pallas_call(
        functools.partial(outer_kernel, width),
        out_shape=jax.ShapeDtypeStruct((share // 2 * sequences, 2 * width), F32),
        in_specs=[VMEM] * (2 + len(messages)),
        out_specs=VMEM,
        scratch_shapes=[pltpu.VMEM((tokens // BLK, share, BLK), F32)],
        compiler_params=PARAMS,
        name="outer_products",
    )(own, other, *messages)


def fisher_kernel(wid_count, *refs):
    seq_count = len(refs) - 3 - wid_count
    gathered = refs[:seq_count]
    high, low = refs[seq_count : seq_count + 2]
    outs = refs[seq_count + 2 : seq_count + 2 + wid_count]
    placed = refs[-1]
    seq = lax.axis_index("seq")
    wid = lax.axis_index("wid")
    per_wid = seq_count // wid_count
    sequences = placed.shape[2]
    steps = gathered[0].shape[0] // sequences
    rows = []
    for ref in gathered:
        rows.append(
            jnp.concatenate(
                [ref[step * sequences : (step + 1) * sequences, :] for step in range(steps)], axis=1
            )
        )
    left_high, left_low = two_parts(jnp.concatenate(rows, axis=0))
    both = jnp.concatenate([left_high, left_low], axis=0)
    count = left_high.shape[0]
    main = lax.dot_general(both, high[...], NT, preferred_element_type=F32)
    rest = lax.dot_general(left_high, low[...], NT, preferred_element_type=F32)
    result = main[:count] + (main[count:] + rest)
    for shift in range(seq_count):
        group = lax.rem(seq - shift + seq_count, seq_count)
        target = lax.rem(group // per_wid - wid + wid_count, wid_count)
        placed[target, lax.rem(group, per_wid)] = result[shift * sequences : (shift + 1) * sequences]
    for target, out in enumerate(outs):
        for group in range(per_wid):
            out[group * sequences : (group + 1) * sequences, 0, :] = placed[target, group]


def fisher_product(gathered, high, low, wid_count):
    seq_count = len(gathered)
    rows, columns = high.shape
    sequences = gathered[0].shape[0] * BLK // columns
    per_wid = seq_count // wid_count
    shape = jax.ShapeDtypeStruct((per_wid * sequences, 1, rows), F32)
    return pl.pallas_call(
        functools.partial(fisher_kernel, wid_count),
        out_shape=[shape] * wid_count,
        in_specs=[VMEM] * (seq_count + 2),
        out_specs=[VMEM] * wid_count,
        scratch_shapes=[pltpu.VMEM((wid_count, per_wid, sequences, rows), F32)],
        compiler_params=PARAMS,
        name="fisher_product",
    )(*gathered, high, low)


def shifted(value, axis, shift):
    count = lax.axis_size(axis)
    return lax.ppermute(value, axis, [(i, (i + shift) % count) for i in range(count)])


def shards(
    activations,
    output_grads,
    act_exponents,
    grad_exponents,
    input_blocks,
    input_index,
    output_blocks,
    output_index,
    fisher_inverse,
):
    seq_count = lax.axis_size("seq")
    wid_count = lax.axis_size("wid")
    pairs = activations.shape[0] // LEN // 2
    indices = (input_index, output_index)
    exponents = (act_exponents, grad_exponents)
    blocks = (jnp.swapaxes(input_blocks, 1, 2), jnp.swapaxes(output_blocks, 1, 2))
    values = tuple(v.reshape(pairs, 2, LEN, v.shape[1]) for v in (activations, output_grads))
    sent = project(True, indices, exponents, blocks, values)
    other = shifted(sent, "rep", 1)
    own = project(False, indices, exponents, blocks, values)
    messages = make_messages(own, other, wid_count)
    messages = [shifted(m, "wid", shift) for shift, m in enumerate(messages, 1)]
    high, low = split_fisher(fisher_inverse)
    outer = outer_products(own, other, messages)
    gathered = [outer] + [shifted(outer, "seq", shift) for shift in range(1, seq_count)]
    parts = fisher_product(gathered, high, low, wid_count)
    result = parts[0]
    for shift in range(1, wid_count):
        result = result + shifted(parts[shift], "wid", shift)
    return result


def solution(mesh):
    placed = (
        P(("grp", "seq"), ("wid", "rep")),
        P(("grp", "seq"), ("wid", "rep")),
        P(("grp", "seq"), ("wid", "rep")),
        P(("grp", "seq"), ("wid", "rep")),
        P(("wid", "rep"), None, None),
        P(("wid", "rep")),
        P(("wid", "rep"), None, None),
        P(("wid", "rep")),
        P("seq", "wid"),
    )
    return jax.shard_map(
        shards,
        mesh=mesh,
        in_specs=placed,
        out_specs=P(("grp", "wid"), "rep", "seq"),
        check_vma=False,
    )
```

```python
import functools

import jax
import jax.numpy as jnp
from jax import lax
from jax.experimental import pallas as pl
from jax.experimental.pallas import tpu as pltpu
from jax.sharding import PartitionSpec as P

BLK = 128
LEN = 64
NT = (((1,), (1,)), ((), ()))
F32 = jnp.float32
BF16 = jnp.bfloat16
VMEM = pl.BlockSpec(memory_space=pltpu.VMEM)
HBM = pl.BlockSpec(memory_space=pltpu.HBM)
PARAMS = pltpu.CompilerParams(vmem_limit_bytes=16 << 20)


def two_parts(x):
    high = x.astype(BF16)
    return high, (x - high.astype(F32)).astype(BF16)


def product(left, right, dims):
    left_high, left_low = two_parts(left)
    right_high, right_low = two_parts(right)
    dot = functools.partial(lax.dot_general, dimension_numbers=dims, preferred_element_type=F32)
    return dot(left_high, right_high) + (dot(left_high, right_low) + dot(left_low, right_high))


def scaled_rows(rows, scale):
    return rows * jnp.concatenate([scale] * (rows.shape[0] // scale.shape[0]), axis=0)


def project_side(picked, scale_of, weights, side):
    _, chosen, pairs, _, _ = picked.shape
    tokens = jnp.concatenate(
        [
            jnp.concatenate(
                [scaled_rows(picked[side, block, pair], scale_of(block, pair)) for pair in range(pairs)],
                axis=0,
            )
            for block in range(chosen)
        ],
        axis=1,
    )
    factor = jnp.concatenate([weights[side, block] for block in range(chosen)], axis=1)
    return lax.dot_general(factor, tokens, NT, preferred_element_type=F32)


def project_other_kernel(
    act_index,
    grad_index,
    act_exponents,
    grad_exponents,
    act_blocks,
    grad_blocks,
    acts,
    grads,
    sent,
    picked_own,
    scales_own,
    weights,
    index,
    exponents,
    picked_other,
    small_sems,
    sems,
):
    own = lax.axis_index("rep")
    other = 1 - own
    _, chosen, pairs, _, _ = picked_own.shape
    block_count = exponents.shape[2]
    values = (acts, grads)
    small = []
    for place, (sources, target) in enumerate(
        (
            ((act_index, grad_index), index),
            ((act_exponents, grad_exponents), exponents),
            ((act_blocks, grad_blocks), weights),
        )
    ):
        for side, source in enumerate(sources):
            copy = pltpu.make_async_copy(source, target.at[side], small_sems.at[place, side])
            copy.start()
            small.append(copy)
    local = []
    for side in range(2):
        small[side].wait()
        local.append([lax.rem(index[side, block], block_count) for block in range(chosen)])
    copies = {}
    for place, (parity, target) in enumerate(((other, picked_other), (own, picked_own))):
        for side in range(2):
            for block in range(chosen):
                columns = pl.ds(pl.multiple_of(local[side][block] * BLK, BLK), BLK)
                copy = pltpu.make_async_copy(
                    values[side].at[:, parity, :, columns],
                    target.at[side, block],
                    sems.at[place, side, block],
                )
                copy.start()
                copies[place, side, block] = copy
    for copy in small[2:]:
        copy.wait()

    def scale_of(side, block, pair, parity):
        exponent = exponents[side, 2 * pair + parity, local[side][block]]
        return jnp.exp2(jnp.full((16, BLK), exponent, jnp.int32).astype(F32)).astype(BF16)

    for side in range(2):
        for block in range(chosen):
            for pair in range(pairs):
                scales_own[side, block, pair] = scale_of(side, block, pair, own)
    width = weights.shape[2]
    for side in range(2):
        for block in range(chosen):
            copies[0, side, block].wait()
        sent[side * width : (side + 1) * width, :] = project_side(
            picked_other, lambda block, pair: scale_of(side, block, pair, other), weights, side
        )
    for side in range(2):
        for block in range(chosen):
            copies[1, side, block].wait()


def project_other(indices, exponents, blocks, values):
    pairs, _, _, features = values[0].shape
    chosen, width, _ = blocks[0].shape
    tokens = pairs * LEN
    operands = [
        pltpu.with_memory_space_constraint(v, pltpu.HBM)
        for v in (*indices, *exponents, *blocks, *values)
    ]
    return pl.pallas_call(
        project_other_kernel,
        out_shape=(
            jax.ShapeDtypeStruct((2 * width, tokens), F32),
            jax.ShapeDtypeStruct((2, chosen, pairs, LEN, BLK), BF16),
            jax.ShapeDtypeStruct((2, chosen, pairs, 16, BLK), BF16),
            jax.ShapeDtypeStruct((2, chosen, width, BLK), BF16),
        ),
        in_specs=[HBM] * 8,
        out_specs=[VMEM] * 4,
        scratch_shapes=[
            pltpu.SMEM((2, chosen), jnp.int32),
            pltpu.SMEM((2, *exponents[0].shape), jnp.int32),
            pltpu.VMEM((2, chosen, pairs, LEN, BLK), BF16),
            pltpu.SemaphoreType.DMA((3, 2)),
            pltpu.SemaphoreType.DMA((2, 2, chosen)),
        ],
        cost_estimate=pl.CostEstimate(
            flops=4 * tokens * chosen * BLK * width,
            bytes_accessed=8 * tokens * chosen * BLK + 8 * tokens * width,
            transcendentals=0,
        ),
        compiler_params=PARAMS,
        name="project_other",
    )(*operands)


def project_own_kernel(picked, scales, weights, out):
    width = weights.shape[2]
    for side in range(2):
        out[side * width : (side + 1) * width, :] = project_side(
            picked, lambda block, pair: scales[side, block, pair], weights, side
        )


def project_own(picked, scales, weights):
    _, chosen, pairs, _, _ = picked.shape
    width = weights.shape[2]
    tokens = pairs * LEN
    return pl.pallas_call(
        project_own_kernel,
        out_shape=jax.ShapeDtypeStruct((2 * width, tokens), F32),
        in_specs=[VMEM] * 3,
        out_specs=VMEM,
        cost_estimate=pl.CostEstimate(
            flops=4 * tokens * chosen * BLK * width,
            bytes_accessed=4 * tokens * chosen * BLK + 8 * tokens * width,
            transcendentals=0,
        ),
        compiler_params=PARAMS,
        name="project_own",
    )(picked, scales, weights)


def split_kernel(fisher, high, low, held, sems):
    pieces = held.shape[0]
    rows = fisher.shape[0] // pieces
    copies = [
        pltpu.make_async_copy(fisher.at[pl.ds(piece * rows, rows)], held.at[piece], sems.at[piece])
        for piece in range(pieces)
    ]
    for copy in copies:
        copy.start()
    for piece in range(pieces):
        copies[piece].wait()

        @pl.loop(0, rows // 16)
        def _(step):
            part_high, part_low = two_parts(held[piece, pl.ds(step * 16, 16), :])
            target = pl.ds(piece * rows + step * 16, 16)
            high[target, :] = part_high
            low[target, :] = part_low


def split_fisher(fisher):
    rows, columns = fisher.shape
    pieces = 8
    half = jax.ShapeDtypeStruct((rows, columns), BF16)
    return pl.pallas_call(
        split_kernel,
        out_shape=(half, half),
        in_specs=[HBM],
        out_specs=(VMEM, VMEM),
        scratch_shapes=[
            pltpu.VMEM((pieces, rows // pieces, columns), F32),
            pltpu.SemaphoreType.DMA((pieces,)),
        ],
        cost_estimate=pl.CostEstimate(
            flops=2 * rows * columns, bytes_accessed=8 * rows * columns, transcendentals=0
        ),
        compiler_params=PARAMS,
        name="split_fisher",
    )(pltpu.with_memory_space_constraint(fisher, pltpu.HBM))


def message_kernel(width, own, other, *messages):
    wid = lax.axis_index("wid")
    count = len(messages) + 1
    share = width // count
    acts = own[:width, :] + other[:width, :]
    for shift, message in enumerate(messages, 1):
        target = lax.rem(wid + shift, count)
        rows = pl.ds(pl.multiple_of(width + target * share, share), share)
        message[:width, :] = acts
        message[width:, :] = own[rows, :] + other[rows, :]


def make_messages(own, other, wid_count):
    width = own.shape[0] // 2
    shape = jax.ShapeDtypeStruct((width + width // wid_count, own.shape[1]), F32)
    return pl.pallas_call(
        functools.partial(message_kernel, width),
        out_shape=[shape] * (wid_count - 1),
        in_specs=[VMEM] * 2,
        out_specs=[VMEM] * (wid_count - 1),
        compiler_params=PARAMS,
        name="make_messages",
    )(own, other)


def outer_kernel(width, own, other, *rest):
    *messages, out, staged = rest
    wid = lax.axis_index("wid")
    share = width // (len(messages) + 1)
    rows = pl.ds(pl.multiple_of(width + wid * share, share), share)
    acts = own[:width, :] + other[:width, :]
    grads = own[rows, :] + other[rows, :]
    for message in messages:
        acts = acts + message[:width, :]
        grads = grads + message[width:, :]
    half = share // 2
    pairs = acts.shape[1] // BLK
    lane = lax.broadcasted_iota(jnp.int32, (half, BLK), 1)
    for pair in range(pairs):
        columns = slice(pair * BLK, (pair + 1) * BLK)
        staged[pair] = grads[:, columns]
        pieces = []
        for odd in range(2):
            part = staged[pair, pl.ds(odd, half, stride=2), :]
            pieces.append(jnp.where(lane < LEN, part, 0.0))
            pieces.append(jnp.where(lane < LEN, 0.0, part))
        left = jnp.concatenate(pieces, axis=0)
        result = product(left, acts[:, columns], NT) * (1.0 / LEN)
        both = jnp.concatenate([result[: 2 * half, :], result[2 * half :, :]], axis=1)
        out[pl.ds(2 * pair, half, stride=2 * pairs), :] = both[:half, :]
        out[pl.ds(2 * pair + 1, half, stride=2 * pairs), :] = both[half:, :]


def outer_products(own, other, messages):
    width = own.shape[0] // 2
    tokens = own.shape[1]
    share = width // (len(messages) + 1)
    sequences = tokens // LEN
    return pl.pallas_call(
        functools.partial(outer_kernel, width),
        out_shape=jax.ShapeDtypeStruct((share // 2 * sequences, 2 * width), F32),
        in_specs=[VMEM] * (2 + len(messages)),
        out_specs=VMEM,
        scratch_shapes=[pltpu.VMEM((tokens // BLK, share, BLK), F32)],
        compiler_params=PARAMS,
        name="outer_products",
    )(own, other, *messages)


def fisher_kernel(wid_count, *refs):
    seq_count = len(refs) - 3 - wid_count
    gathered = refs[:seq_count]
    high, low = refs[seq_count : seq_count + 2]
    outs = refs[seq_count + 2 : seq_count + 2 + wid_count]
    placed = refs[-1]
    seq = lax.axis_index("seq")
    wid = lax.axis_index("wid")
    per_wid = seq_count // wid_count
    sequences = placed.shape[2]
    steps = gathered[0].shape[0] // sequences
    rows = []
    for ref in gathered:
        rows.append(
            jnp.concatenate(
                [ref[step * sequences : (step + 1) * sequences, :] for step in range(steps)], axis=1
            )
        )
    left_high, left_low = two_parts(jnp.concatenate(rows, axis=0))
    both = jnp.concatenate([left_high, left_low], axis=0)
    count = left_high.shape[0]
    main = lax.dot_general(both, high[...], NT, preferred_element_type=F32)
    rest = lax.dot_general(left_high, low[...], NT, preferred_element_type=F32)
    result = main[:count] + (main[count:] + rest)
    for shift in range(seq_count):
        group = seq ^ shift
        target = lax.rem(group // per_wid - wid + wid_count, wid_count)
        placed[target, lax.rem(group, per_wid)] = result[shift * sequences : (shift + 1) * sequences]
    for target, out in enumerate(outs):
        for group in range(per_wid):
            out[group * sequences : (group + 1) * sequences, 0, :] = placed[target, group]


def fisher_product(gathered, high, low, wid_count):
    seq_count = len(gathered)
    rows, columns = high.shape
    sequences = gathered[0].shape[0] * BLK // columns
    per_wid = seq_count // wid_count
    shape = jax.ShapeDtypeStruct((per_wid * sequences, 1, rows), F32)
    return pl.pallas_call(
        functools.partial(fisher_kernel, wid_count),
        out_shape=[shape] * wid_count,
        in_specs=[VMEM] * (seq_count + 2),
        out_specs=[VMEM] * wid_count,
        scratch_shapes=[pltpu.VMEM((wid_count, per_wid, sequences, rows), F32)],
        compiler_params=PARAMS,
        name="fisher_product",
    )(*gathered, high, low)


def shifted(value, axis, shift):
    count = lax.axis_size(axis)
    return lax.ppermute(value, axis, [(i, (i + shift) % count) for i in range(count)])


def swapped(value, axis, step):
    return lax.ppermute(value, axis, [(i, i ^ step) for i in range(lax.axis_size(axis))])


def shards(
    activations,
    output_grads,
    act_exponents,
    grad_exponents,
    input_blocks,
    input_index,
    output_blocks,
    output_index,
    fisher_inverse,
):
    seq_count = lax.axis_size("seq")
    wid_count = lax.axis_size("wid")
    pairs = activations.shape[0] // LEN // 2
    indices = (input_index, output_index)
    exponents = (act_exponents, grad_exponents)
    blocks = (jnp.swapaxes(input_blocks, 1, 2), jnp.swapaxes(output_blocks, 1, 2))
    values = tuple(v.reshape(pairs, 2, LEN, v.shape[1]) for v in (activations, output_grads))
    sent, *held = project_other(indices, exponents, blocks, values)
    other = shifted(sent, "rep", 1)
    own = project_own(*held)
    messages = make_messages(own, other, wid_count)
    fisher_inverse, *messages = lax.optimization_barrier((fisher_inverse, *messages))
    received = [shifted(m, "wid", shift) for shift, m in enumerate(messages, 1)]
    high, low = split_fisher(fisher_inverse)
    own, high, low = lax.optimization_barrier((own, high, low))
    outer = outer_products(own, other, received)
    gathered = [outer] + [swapped(outer, "seq", step) for step in range(1, seq_count)]
    parts = fisher_product(gathered, high, low, wid_count)
    result = parts[0]
    for shift in range(1, wid_count):
        result = result + shifted(parts[shift], "wid", shift)
    return result


def solution(mesh):
    placed = (
        P(("grp", "seq"), ("wid", "rep")),
        P(("grp", "seq"), ("wid", "rep")),
        P(("grp", "seq"), ("wid", "rep")),
        P(("grp", "seq"), ("wid", "rep")),
        P(("wid", "rep"), None, None),
        P(("wid", "rep")),
        P(("wid", "rep"), None, None),
        P(("wid", "rep")),
        P("seq", "wid"),
    )
    return jax.shard_map(
        shards,
        mesh=mesh,
        in_specs=placed,
        out_specs=P(("grp", "wid"), "rep", "seq"),
        check_vma=False,
    )
```

```python
import functools

import jax
import jax.numpy as jnp
from jax import lax
from jax.experimental import pallas as pl
from jax.experimental.pallas import tpu as pltpu
from jax.sharding import PartitionSpec as P

BLK = 128
LEN = 64
MXU = 256
NT = (((1,), (1,)), ((), ()))
F32 = jnp.float32
BF16 = jnp.bfloat16
VMEM = pl.BlockSpec(memory_space=pltpu.VMEM)
HBM = pl.BlockSpec(memory_space=pltpu.HBM)
PARAMS = pltpu.CompilerParams(vmem_limit_bytes=16 << 20)


def two_parts(x):
    high = x.astype(BF16)
    return high, (x - high.astype(F32)).astype(BF16)


def product(left, right, dims):
    left_high, left_low = two_parts(left)
    right_high, right_low = two_parts(right)
    dot = functools.partial(lax.dot_general, dimension_numbers=dims, preferred_element_type=F32)
    return dot(left_high, right_high) + (dot(left_high, right_low) + dot(left_low, right_high))


def scaled_rows(rows, scale):
    return rows * jnp.concatenate([scale] * (rows.shape[0] // scale.shape[0]), axis=0)


def project_side(picked, scale_of, weights, side):
    _, chosen, pairs, _, _ = picked.shape
    tokens = jnp.concatenate(
        [
            jnp.concatenate(
                [scaled_rows(picked[side, block, pair], scale_of(block, pair)) for pair in range(pairs)],
                axis=0,
            )
            for block in range(chosen)
        ],
        axis=1,
    )
    factor = jnp.concatenate([weights[side, block] for block in range(chosen)], axis=1)
    return lax.dot_general(factor, tokens, NT, preferred_element_type=F32)


def project_other_kernel(
    act_index,
    grad_index,
    act_exponents,
    grad_exponents,
    act_blocks,
    grad_blocks,
    acts,
    grads,
    sent,
    picked_own,
    scales_own,
    weights,
    index,
    exponents,
    picked_other,
    small_sems,
    sems,
):
    own = lax.axis_index("rep")
    other = 1 - own
    _, chosen, pairs, _, _ = picked_own.shape
    block_count = exponents.shape[2]
    values = (acts, grads)
    small = []
    for place, (sources, target) in enumerate(
        (
            ((act_index, grad_index), index),
            ((act_exponents, grad_exponents), exponents),
            ((act_blocks, grad_blocks), weights),
        )
    ):
        for side, source in enumerate(sources):
            copy = pltpu.make_async_copy(source, target.at[side], small_sems.at[place, side])
            copy.start()
            small.append(copy)
    local = []
    for side in range(2):
        small[side].wait()
        local.append([lax.rem(index[side, block], block_count) for block in range(chosen)])
    copies = {}
    for place, (parity, target) in enumerate(((other, picked_other), (own, picked_own))):
        for side in range(2):
            for block in range(chosen):
                columns = pl.ds(pl.multiple_of(local[side][block] * BLK, BLK), BLK)
                copy = pltpu.make_async_copy(
                    values[side].at[:, parity, :, columns],
                    target.at[side, block],
                    sems.at[place, side, block],
                )
                copy.start()
                copies[place, side, block] = copy
    for copy in small[2:]:
        copy.wait()

    def scale_of(side, block, pair, parity):
        exponent = exponents[side, 2 * pair + parity, local[side][block]]
        return jnp.exp2(jnp.full((16, BLK), exponent, jnp.int32).astype(F32)).astype(BF16)

    for side in range(2):
        for block in range(chosen):
            for pair in range(pairs):
                scales_own[side, block, pair] = scale_of(side, block, pair, own)
    width = weights.shape[2]
    for side in range(2):
        for block in range(chosen):
            copies[0, side, block].wait()
        sent[side * width : (side + 1) * width, :] = project_side(
            picked_other, lambda block, pair: scale_of(side, block, pair, other), weights, side
        )
    for side in range(2):
        for block in range(chosen):
            copies[1, side, block].wait()


def project_other(indices, exponents, blocks, values):
    pairs, _, _, features = values[0].shape
    chosen, width, _ = blocks[0].shape
    tokens = pairs * LEN
    operands = [
        pltpu.with_memory_space_constraint(v, pltpu.HBM)
        for v in (*indices, *exponents, *blocks, *values)
    ]
    return pl.pallas_call(
        project_other_kernel,
        out_shape=(
            jax.ShapeDtypeStruct((2 * width, tokens), F32),
            jax.ShapeDtypeStruct((2, chosen, pairs, LEN, BLK), BF16),
            jax.ShapeDtypeStruct((2, chosen, pairs, 16, BLK), BF16),
            jax.ShapeDtypeStruct((2, chosen, width, BLK), BF16),
        ),
        in_specs=[HBM] * 8,
        out_specs=[VMEM] * 4,
        scratch_shapes=[
            pltpu.SMEM((2, chosen), jnp.int32),
            pltpu.SMEM((2, *exponents[0].shape), jnp.int32),
            pltpu.VMEM((2, chosen, pairs, LEN, BLK), BF16),
            pltpu.SemaphoreType.DMA((3, 2)),
            pltpu.SemaphoreType.DMA((2, 2, chosen)),
        ],
        cost_estimate=pl.CostEstimate(
            flops=4 * tokens * chosen * BLK * width,
            bytes_accessed=8 * tokens * chosen * BLK + 8 * tokens * width,
            transcendentals=0,
        ),
        compiler_params=PARAMS,
        name="project_other",
    )(*operands)


def project_own_kernel(picked, scales, weights, out):
    width = weights.shape[2]
    for side in range(2):
        out[side * width : (side + 1) * width, :] = project_side(
            picked, lambda block, pair: scales[side, block, pair], weights, side
        )


def project_own(picked, scales, weights):
    _, chosen, pairs, _, _ = picked.shape
    width = weights.shape[2]
    tokens = pairs * LEN
    return pl.pallas_call(
        project_own_kernel,
        out_shape=jax.ShapeDtypeStruct((2 * width, tokens), F32),
        in_specs=[VMEM] * 3,
        out_specs=VMEM,
        cost_estimate=pl.CostEstimate(
            flops=4 * tokens * chosen * BLK * width,
            bytes_accessed=4 * tokens * chosen * BLK + 8 * tokens * width,
            transcendentals=0,
        ),
        compiler_params=PARAMS,
        name="project_own",
    )(picked, scales, weights)


def split_kernel(fisher, high, low, held, sems):
    pieces = held.shape[0]
    rows = fisher.shape[0] // pieces
    copies = [
        pltpu.make_async_copy(fisher.at[pl.ds(piece * rows, rows)], held.at[piece], sems.at[piece])
        for piece in range(pieces)
    ]
    for copy in copies:
        copy.start()
    for piece in range(pieces):
        copies[piece].wait()

        @pl.loop(0, rows // 16)
        def _(step):
            part_high, part_low = two_parts(held[piece, pl.ds(step * 16, 16), :])
            target = pl.ds(piece * rows + step * 16, 16)
            high[target, :] = part_high
            low[target, :] = part_low


def split_fisher(fisher):
    rows, columns = fisher.shape
    pieces = 8
    half = jax.ShapeDtypeStruct((rows, columns), BF16)
    return pl.pallas_call(
        split_kernel,
        out_shape=(half, half),
        in_specs=[HBM],
        out_specs=(VMEM, VMEM),
        scratch_shapes=[
            pltpu.VMEM((pieces, rows // pieces, columns), F32),
            pltpu.SemaphoreType.DMA((pieces,)),
        ],
        cost_estimate=pl.CostEstimate(
            flops=2 * rows * columns, bytes_accessed=8 * rows * columns, transcendentals=0
        ),
        compiler_params=PARAMS,
        name="split_fisher",
    )(pltpu.with_memory_space_constraint(fisher, pltpu.HBM))


def message_kernel(width, own, other, *messages):
    wid = lax.axis_index("wid")
    count = len(messages) + 1
    share = width // count
    acts = own[:width, :] + other[:width, :]
    for shift, message in enumerate(messages, 1):
        target = lax.rem(wid + shift, count)
        rows = pl.ds(pl.multiple_of(width + target * share, share), share)
        message[:width, :] = acts
        message[width:, :] = own[rows, :] + other[rows, :]


def make_messages(own, other, wid_count):
    width = own.shape[0] // 2
    shape = jax.ShapeDtypeStruct((width + width // wid_count, own.shape[1]), F32)
    return pl.pallas_call(
        functools.partial(message_kernel, width),
        out_shape=[shape] * (wid_count - 1),
        in_specs=[VMEM] * 2,
        out_specs=[VMEM] * (wid_count - 1),
        compiler_params=PARAMS,
        name="make_messages",
    )(own, other)


def outer_kernel(width, own, other, *rest):
    *messages, out, staged = rest
    wid = lax.axis_index("wid")
    share = width // (len(messages) + 1)
    rows = pl.ds(pl.multiple_of(width + wid * share, share), share)
    acts = own[:width, :] + other[:width, :]
    grads = own[rows, :] + other[rows, :]
    for message in messages:
        acts = acts + message[:width, :]
        grads = grads + message[width:, :]
    half = share // 2
    pairs = acts.shape[1] // BLK
    lane = lax.broadcasted_iota(jnp.int32, (half, BLK), 1)
    for pair in range(pairs):
        columns = slice(pair * BLK, (pair + 1) * BLK)
        staged[pair] = grads[:, columns]
        pieces = []
        for odd in range(2):
            part = staged[pair, pl.ds(odd, half, stride=2), :]
            pieces.append(jnp.where(lane < LEN, part, 0.0))
            pieces.append(jnp.where(lane < LEN, 0.0, part))
        left = jnp.concatenate(pieces, axis=0)
        result = product(left, acts[:, columns], NT) * (1.0 / LEN)
        both = jnp.concatenate([result[: 2 * half, :], result[2 * half :, :]], axis=1)
        out[pl.ds(2 * pair, half, stride=2 * pairs), :] = both[:half, :]
        out[pl.ds(2 * pair + 1, half, stride=2 * pairs), :] = both[half:, :]


def outer_products(own, other, messages):
    width = own.shape[0] // 2
    tokens = own.shape[1]
    share = width // (len(messages) + 1)
    sequences = tokens // LEN
    return pl.pallas_call(
        functools.partial(outer_kernel, width),
        out_shape=jax.ShapeDtypeStruct((share // 2 * sequences, 2 * width), F32),
        in_specs=[VMEM] * (2 + len(messages)),
        out_specs=VMEM,
        scratch_shapes=[pltpu.VMEM((tokens // BLK, share, BLK), F32)],
        compiler_params=PARAMS,
        name="outer_products",
    )(own, other, *messages)


def tile_products(left_high, left_low, high, low):
    rows, columns = high.shape
    streamed = rows // 4 // MXU * MXU
    count = left_high.shape[0]
    both = jnp.concatenate([left_high, left_low], axis=0)
    dot = functools.partial(lax.dot_general, dimension_numbers=NT, preferred_element_type=F32)
    sums = None
    for start in range(0, columns, MXU):
        piece = slice(start, start + MXU)
        terms = []
        if streamed:
            terms.append(dot(high[:streamed, piece], both[:, piece]))
        terms.append(dot(both[:, piece], high[streamed:, piece]))
        if streamed:
            terms.append(dot(low[:streamed, piece], left_high[:, piece]))
        terms.append(dot(left_high[:, piece], low[streamed:, piece]))
        sums = terms if sums is None else [a + b for a, b in zip(sums, terms)]
    held_high, held_low = sums[1::2] if streamed else sums
    result = held_high[:count] + (held_high[count:] + held_low)
    if streamed:
        tall = sums[0][:, :count] + (sums[0][:, count:] + sums[2])
        result = jnp.concatenate([tall.T, result], axis=1)
    return result


def fisher_kernel(wid_count, *refs):
    seq_count = len(refs) - 3 - wid_count
    gathered = refs[:seq_count]
    high, low = refs[seq_count : seq_count + 2]
    outs = refs[seq_count + 2 : seq_count + 2 + wid_count]
    placed = refs[-1]
    seq = lax.axis_index("seq")
    wid = lax.axis_index("wid")
    per_wid = seq_count // wid_count
    sequences = placed.shape[2]
    steps = gathered[0].shape[0] // sequences
    rows = []
    for ref in gathered:
        rows.append(
            jnp.concatenate(
                [ref[step * sequences : (step + 1) * sequences, :] for step in range(steps)], axis=1
            )
        )
    left_high, left_low = two_parts(jnp.concatenate(rows, axis=0))
    result = tile_products(left_high, left_low, high, low)
    for shift in range(seq_count):
        group = seq ^ shift
        target = lax.rem(group // per_wid - wid + wid_count, wid_count)
        placed[target, lax.rem(group, per_wid)] = result[shift * sequences : (shift + 1) * sequences]
    for target, out in enumerate(outs):
        for group in range(per_wid):
            out[group * sequences : (group + 1) * sequences, 0, :] = placed[target, group]


def fisher_product(gathered, high, low, wid_count):
    seq_count = len(gathered)
    rows, columns = high.shape
    sequences = gathered[0].shape[0] * BLK // columns
    per_wid = seq_count // wid_count
    shape = jax.ShapeDtypeStruct((per_wid * sequences, 1, rows), F32)
    return pl.pallas_call(
        functools.partial(fisher_kernel, wid_count),
        out_shape=[shape] * wid_count,
        in_specs=[VMEM] * (seq_count + 2),
        out_specs=[VMEM] * wid_count,
        scratch_shapes=[pltpu.VMEM((wid_count, per_wid, sequences, rows), F32)],
        compiler_params=PARAMS,
        name="fisher_product",
    )(*gathered, high, low)


def shifted(value, axis, shift):
    count = lax.axis_size(axis)
    return lax.ppermute(value, axis, [(i, (i + shift) % count) for i in range(count)])


def swapped(value, axis, step):
    return lax.ppermute(value, axis, [(i, i ^ step) for i in range(lax.axis_size(axis))])


def shards(
    activations,
    output_grads,
    act_exponents,
    grad_exponents,
    input_blocks,
    input_index,
    output_blocks,
    output_index,
    fisher_inverse,
):
    seq_count = lax.axis_size("seq")
    wid_count = lax.axis_size("wid")
    pairs = activations.shape[0] // LEN // 2
    indices = (input_index, output_index)
    exponents = (act_exponents, grad_exponents)
    blocks = (jnp.swapaxes(input_blocks, 1, 2), jnp.swapaxes(output_blocks, 1, 2))
    values = tuple(v.reshape(pairs, 2, LEN, v.shape[1]) for v in (activations, output_grads))
    sent, *held = project_other(indices, exponents, blocks, values)
    other = shifted(sent, "rep", 1)
    own = project_own(*held)
    messages = make_messages(own, other, wid_count)
    fisher_inverse, *messages = lax.optimization_barrier((fisher_inverse, *messages))
    received = [shifted(m, "wid", shift) for shift, m in enumerate(messages, 1)]
    high, low = split_fisher(fisher_inverse)
    own, high, low = lax.optimization_barrier((own, high, low))
    outer = outer_products(own, other, received)
    gathered = [outer] + [swapped(outer, "seq", step) for step in range(1, seq_count)]
    parts = fisher_product(gathered, high, low, wid_count)
    result = parts[0]
    for shift in range(1, wid_count):
        result = result + shifted(parts[shift], "wid", shift)
    return result


def solution(mesh):
    placed = (
        P(("grp", "seq"), ("wid", "rep")),
        P(("grp", "seq"), ("wid", "rep")),
        P(("grp", "seq"), ("wid", "rep")),
        P(("grp", "seq"), ("wid", "rep")),
        P(("wid", "rep"), None, None),
        P(("wid", "rep")),
        P(("wid", "rep"), None, None),
        P(("wid", "rep")),
        P("seq", "wid"),
    )
    return jax.shard_map(
        shards,
        mesh=mesh,
        in_specs=placed,
        out_specs=P(("grp", "wid"), "rep", "seq"),
        check_vma=False,
    )
```

```python
import functools

import jax
import jax.numpy as jnp
from jax import lax
from jax.experimental import pallas as pl
from jax.experimental.pallas import tpu as pltpu
from jax.sharding import PartitionSpec as P

BLK = 128
LEN = 64
MXU = 256
PIECES = 8
NT = (((1,), (1,)), ((), ()))
F32 = jnp.float32
BF16 = jnp.bfloat16
VMEM = pl.BlockSpec(memory_space=pltpu.VMEM)
HBM = pl.BlockSpec(memory_space=pltpu.HBM)
PARAMS = pltpu.CompilerParams(vmem_limit_bytes=16 << 20)


def two_parts(x):
    high = x.astype(BF16)
    return high, (x - high.astype(F32)).astype(BF16)


def product(left, right, dims):
    left_high, left_low = two_parts(left)
    right_high, right_low = two_parts(right)
    dot = functools.partial(lax.dot_general, dimension_numbers=dims, preferred_element_type=F32)
    return dot(left_high, right_high) + (dot(left_high, right_low) + dot(left_low, right_high))


def scaled_rows(rows, scale):
    return rows * jnp.concatenate([scale] * (rows.shape[0] // scale.shape[0]), axis=0)


def project_side(picked, scale_of, weights, side):
    _, chosen, pairs, _, _ = picked.shape
    tokens = jnp.concatenate(
        [
            jnp.concatenate(
                [scaled_rows(picked[side, block, pair], scale_of(block, pair)) for pair in range(pairs)],
                axis=0,
            )
            for block in range(chosen)
        ],
        axis=1,
    )
    factor = jnp.concatenate([weights[side, block] for block in range(chosen)], axis=1)
    return lax.dot_general(factor, tokens, NT, preferred_element_type=F32)


def project_other_kernel(
    act_index,
    grad_index,
    act_exponents,
    grad_exponents,
    act_blocks,
    grad_blocks,
    acts,
    grads,
    sent,
    picked_own,
    scales_own,
    weights,
    index,
    exponents,
    picked_other,
    small_sems,
    sems,
):
    own = lax.axis_index("rep")
    other = 1 - own
    _, chosen, pairs, _, _ = picked_own.shape
    block_count = exponents.shape[2]
    values = (acts, grads)
    small = []
    for place, (sources, target) in enumerate(
        (
            ((act_index, grad_index), index),
            ((act_exponents, grad_exponents), exponents),
            ((act_blocks, grad_blocks), weights),
        )
    ):
        for side, source in enumerate(sources):
            copy = pltpu.make_async_copy(source, target.at[side], small_sems.at[place, side])
            copy.start()
            small.append(copy)
    local = []
    for side in range(2):
        small[side].wait()
        local.append([lax.rem(index[side, block], block_count) for block in range(chosen)])
    copies = {}
    for place, (parity, target) in enumerate(((other, picked_other), (own, picked_own))):
        for side in range(2):
            for block in range(chosen):
                columns = pl.ds(pl.multiple_of(local[side][block] * BLK, BLK), BLK)
                copy = pltpu.make_async_copy(
                    values[side].at[:, parity, :, columns],
                    target.at[side, block],
                    sems.at[place, side, block],
                )
                copy.start()
                copies[place, side, block] = copy
    for copy in small[2:]:
        copy.wait()

    def scale_of(side, block, pair, parity):
        exponent = exponents[side, 2 * pair + parity, local[side][block]]
        return jnp.exp2(jnp.full((16, BLK), exponent, jnp.int32).astype(F32)).astype(BF16)

    for side in range(2):
        for block in range(chosen):
            for pair in range(pairs):
                scales_own[side, block, pair] = scale_of(side, block, pair, own)
    width = weights.shape[2]
    for side in range(2):
        for block in range(chosen):
            copies[0, side, block].wait()
        sent[side * width : (side + 1) * width, :] = project_side(
            picked_other, lambda block, pair: scale_of(side, block, pair, other), weights, side
        )
    for side in range(2):
        for block in range(chosen):
            copies[1, side, block].wait()


def project_other(indices, exponents, blocks, values):
    pairs, _, _, features = values[0].shape
    chosen, width, _ = blocks[0].shape
    tokens = pairs * LEN
    operands = [
        pltpu.with_memory_space_constraint(v, pltpu.HBM)
        for v in (*indices, *exponents, *blocks, *values)
    ]
    return pl.pallas_call(
        project_other_kernel,
        out_shape=(
            jax.ShapeDtypeStruct((2 * width, tokens), F32),
            jax.ShapeDtypeStruct((2, chosen, pairs, LEN, BLK), BF16),
            jax.ShapeDtypeStruct((2, chosen, pairs, 16, BLK), BF16),
            jax.ShapeDtypeStruct((2, chosen, width, BLK), BF16),
        ),
        in_specs=[HBM] * 8,
        out_specs=[VMEM] * 4,
        scratch_shapes=[
            pltpu.SMEM((2, chosen), jnp.int32),
            pltpu.SMEM((2, *exponents[0].shape), jnp.int32),
            pltpu.VMEM((2, chosen, pairs, LEN, BLK), BF16),
            pltpu.SemaphoreType.DMA((3, 2)),
            pltpu.SemaphoreType.DMA((2, 2, chosen)),
        ],
        cost_estimate=pl.CostEstimate(
            flops=4 * tokens * chosen * BLK * width,
            bytes_accessed=8 * tokens * chosen * BLK + 8 * tokens * width,
            transcendentals=0,
        ),
        compiler_params=PARAMS,
        name="project_other",
    )(*operands)


def project_own_kernel(picked, scales, weights, out):
    width = weights.shape[2]
    for side in range(2):
        out[side * width : (side + 1) * width, :] = project_side(
            picked, lambda block, pair: scales[side, block, pair], weights, side
        )


def project_own(picked, scales, weights):
    _, chosen, pairs, _, _ = picked.shape
    width = weights.shape[2]
    tokens = pairs * LEN
    return pl.pallas_call(
        project_own_kernel,
        out_shape=jax.ShapeDtypeStruct((2 * width, tokens), F32),
        in_specs=[VMEM] * 3,
        out_specs=VMEM,
        cost_estimate=pl.CostEstimate(
            flops=4 * tokens * chosen * BLK * width,
            bytes_accessed=4 * tokens * chosen * BLK + 8 * tokens * width,
            transcendentals=0,
        ),
        compiler_params=PARAMS,
        name="project_own",
    )(picked, scales, weights)


def split_pieces(fisher, high, low, held, sems):
    pieces, rows, _ = held.shape
    copies = [
        pltpu.make_async_copy(fisher.at[pl.ds(piece * rows, rows)], held.at[piece], sems.at[piece])
        for piece in range(pieces)
    ]
    for copy in copies:
        copy.start()
    for piece in range(pieces):
        copies[piece].wait()

        @pl.loop(0, rows // 16)
        def _(step):
            part_high, part_low = two_parts(held[piece, pl.ds(step * 16, 16), :])
            target = pl.ds(piece * rows + step * 16, 16)
            high[target, :] = part_high
            low[target, :] = part_low


def split_early_kernel(fisher, high, low, held, sems):
    @pl.when(lax.axis_index("rep") == 1)
    def _():
        split_pieces(fisher, high, low, held, sems)


def split_late_kernel(fisher, high_in, low_in, high, low, held, sems):
    del high_in, low_in

    @pl.when(lax.axis_index("rep") == 0)
    def _():
        split_pieces(fisher, high, low, held, sems)


def split_fisher(fisher, *halves):
    rows, columns = fisher.shape
    half = jax.ShapeDtypeStruct((rows, columns), BF16)
    return pl.pallas_call(
        split_late_kernel if halves else split_early_kernel,
        out_shape=(half, half),
        in_specs=[HBM] + [VMEM] * len(halves),
        out_specs=(VMEM, VMEM),
        scratch_shapes=[
            pltpu.VMEM((PIECES, rows // PIECES, columns), F32),
            pltpu.SemaphoreType.DMA((PIECES,)),
        ],
        input_output_aliases={1: 0, 2: 1} if halves else {},
        cost_estimate=pl.CostEstimate(
            flops=2 * rows * columns, bytes_accessed=8 * rows * columns, transcendentals=0
        ),
        compiler_params=PARAMS,
        name="split_late" if halves else "split_early",
    )(pltpu.with_memory_space_constraint(fisher, pltpu.HBM), *halves)


def message_kernel(width, own, other, *messages):
    wid = lax.axis_index("wid")
    count = len(messages) + 1
    share = width // count
    acts = own[:width, :] + other[:width, :]
    for shift, message in enumerate(messages, 1):
        target = lax.rem(wid + shift, count)
        rows = pl.ds(pl.multiple_of(width + target * share, share), share)
        message[:width, :] = acts
        message[width:, :] = own[rows, :] + other[rows, :]


def make_messages(own, other, wid_count):
    width = own.shape[0] // 2
    shape = jax.ShapeDtypeStruct((width + width // wid_count, own.shape[1]), F32)
    return pl.pallas_call(
        functools.partial(message_kernel, width),
        out_shape=[shape] * (wid_count - 1),
        in_specs=[VMEM] * 2,
        out_specs=[VMEM] * (wid_count - 1),
        compiler_params=PARAMS,
        name="make_messages",
    )(own, other)


def outer_kernel(width, own, other, *rest):
    *messages, out, staged = rest
    wid = lax.axis_index("wid")
    share = width // (len(messages) + 1)
    rows = pl.ds(pl.multiple_of(width + wid * share, share), share)
    acts = own[:width, :] + other[:width, :]
    grads = own[rows, :] + other[rows, :]
    for message in messages:
        acts = acts + message[:width, :]
        grads = grads + message[width:, :]
    half = share // 2
    pairs = acts.shape[1] // BLK
    lane = lax.broadcasted_iota(jnp.int32, (half, BLK), 1)
    for pair in range(pairs):
        columns = slice(pair * BLK, (pair + 1) * BLK)
        staged[pair] = grads[:, columns]
        pieces = []
        for odd in range(2):
            part = staged[pair, pl.ds(odd, half, stride=2), :]
            pieces.append(jnp.where(lane < LEN, part, 0.0))
            pieces.append(jnp.where(lane < LEN, 0.0, part))
        left = jnp.concatenate(pieces, axis=0)
        result = product(left, acts[:, columns], NT) * (1.0 / LEN)
        both = jnp.concatenate([result[: 2 * half, :], result[2 * half :, :]], axis=1)
        out[pl.ds(2 * pair, half, stride=2 * pairs), :] = both[:half, :]
        out[pl.ds(2 * pair + 1, half, stride=2 * pairs), :] = both[half:, :]


def outer_products(own, other, messages):
    width = own.shape[0] // 2
    tokens = own.shape[1]
    share = width // (len(messages) + 1)
    sequences = tokens // LEN
    return pl.pallas_call(
        functools.partial(outer_kernel, width),
        out_shape=jax.ShapeDtypeStruct((share // 2 * sequences, 2 * width), F32),
        in_specs=[VMEM] * (2 + len(messages)),
        out_specs=VMEM,
        scratch_shapes=[pltpu.VMEM((tokens // BLK, share, BLK), F32)],
        compiler_params=PARAMS,
        name="outer_products",
    )(own, other, *messages)


def tile_products(left_high, left_low, high, low):
    rows, columns = high.shape
    streamed = rows // 4 // MXU * MXU
    count = left_high.shape[0]
    both = jnp.concatenate([left_high, left_low], axis=0)
    dot = functools.partial(lax.dot_general, dimension_numbers=NT, preferred_element_type=F32)
    sums = None
    for start in range(0, columns, MXU):
        piece = slice(start, start + MXU)
        terms = []
        if streamed:
            terms.append(dot(high[:streamed, piece], both[:, piece]))
        terms.append(dot(both[:, piece], high[streamed:, piece]))
        if streamed:
            terms.append(dot(low[:streamed, piece], left_high[:, piece]))
        terms.append(dot(left_high[:, piece], low[streamed:, piece]))
        sums = terms if sums is None else [a + b for a, b in zip(sums, terms)]
    held_high, held_low = sums[1::2] if streamed else sums
    result = held_high[:count] + (held_high[count:] + held_low)
    if streamed:
        tall = sums[0][:, :count] + (sums[0][:, count:] + sums[2])
        result = jnp.concatenate([tall.T, result], axis=1)
    return result


def exchange_steps(seq_count):
    steps = range(1, seq_count)
    return list(zip(steps, sorted(steps, key=lambda step: (step.bit_count(), -step))))


def fisher_kernel(wid_count, *refs):
    seq_count = len(refs) - 3 - wid_count
    gathered = refs[:seq_count]
    high, low = refs[seq_count : seq_count + 2]
    outs = refs[seq_count + 2 : seq_count + 2 + wid_count]
    placed = refs[-1]
    seq = lax.axis_index("seq")
    wid = lax.axis_index("wid")
    per_wid = seq_count // wid_count
    sequences = placed.shape[2]
    steps = gathered[0].shape[0] // sequences
    rows = []
    for ref in gathered:
        rows.append(
            jnp.concatenate(
                [ref[step * sequences : (step + 1) * sequences, :] for step in range(steps)], axis=1
            )
        )
    left_high, left_low = two_parts(jnp.concatenate(rows, axis=0))
    result = tile_products(left_high, left_low, high, low)
    rep = lax.axis_index("rep")
    for shift, (first, second) in enumerate([(0, 0)] + exchange_steps(seq_count)):
        group = seq ^ jnp.where(rep == 0, first, second)
        target = lax.rem(group // per_wid - wid + wid_count, wid_count)
        placed[target, lax.rem(group, per_wid)] = result[shift * sequences : (shift + 1) * sequences]
    for target, out in enumerate(outs):
        for group in range(per_wid):
            out[group * sequences : (group + 1) * sequences, 0, :] = placed[target, group]


def fisher_product(gathered, high, low, wid_count):
    seq_count = len(gathered)
    rows, columns = high.shape
    sequences = gathered[0].shape[0] * BLK // columns
    per_wid = seq_count // wid_count
    shape = jax.ShapeDtypeStruct((per_wid * sequences, 1, rows), F32)
    return pl.pallas_call(
        functools.partial(fisher_kernel, wid_count),
        out_shape=[shape] * wid_count,
        in_specs=[VMEM] * (seq_count + 2),
        out_specs=[VMEM] * wid_count,
        scratch_shapes=[pltpu.VMEM((wid_count, per_wid, sequences, rows), F32)],
        compiler_params=PARAMS,
        name="fisher_product",
    )(*gathered, high, low)


def shifted(value, axis, shift):
    count = lax.axis_size(axis)
    return lax.ppermute(value, axis, [(i, (i + shift) % count) for i in range(count)])


def exchanged(value, steps):
    cores = lax.axis_size("rep")
    pairs = [
        (seq * cores + core, (seq ^ steps[core]) * cores + core)
        for seq in range(lax.axis_size("seq"))
        for core in range(cores)
    ]
    return lax.ppermute(value, ("seq", "rep"), pairs)


def shards(
    activations,
    output_grads,
    act_exponents,
    grad_exponents,
    input_blocks,
    input_index,
    output_blocks,
    output_index,
    fisher_inverse,
):
    seq_count = lax.axis_size("seq")
    wid_count = lax.axis_size("wid")
    pairs = activations.shape[0] // LEN // 2
    indices = (input_index, output_index)
    exponents = (act_exponents, grad_exponents)
    blocks = (jnp.swapaxes(input_blocks, 1, 2), jnp.swapaxes(output_blocks, 1, 2))
    values = tuple(v.reshape(pairs, 2, LEN, v.shape[1]) for v in (activations, output_grads))
    sent, *held = project_other(indices, exponents, blocks, values)
    other = shifted(sent, "rep", 1)
    own = project_own(*held)
    fisher, own = lax.optimization_barrier((fisher_inverse, own))
    halves = split_fisher(fisher)
    own, other, *halves = lax.optimization_barrier((own, other, *halves))
    messages = make_messages(own, other, wid_count)
    fisher, *messages = lax.optimization_barrier((fisher, *messages))
    received = [shifted(m, "wid", shift) for shift, m in enumerate(messages, 1)]
    high, low = split_fisher(fisher, *halves)
    own, high, low = lax.optimization_barrier((own, high, low))
    outer = outer_products(own, other, received)
    gathered = [outer] + [exchanged(outer, steps) for steps in exchange_steps(seq_count)]
    parts = fisher_product(gathered, high, low, wid_count)
    result = parts[0]
    for shift in range(1, wid_count):
        result = result + shifted(parts[shift], "wid", shift)
    return result


def solution(mesh):
    placed = (
        P(("grp", "seq"), ("wid", "rep")),
        P(("grp", "seq"), ("wid", "rep")),
        P(("grp", "seq"), ("wid", "rep")),
        P(("grp", "seq"), ("wid", "rep")),
        P(("wid", "rep"), None, None),
        P(("wid", "rep")),
        P(("wid", "rep"), None, None),
        P(("wid", "rep")),
        P("seq", "wid"),
    )
    return jax.shard_map(
        shards,
        mesh=mesh,
        in_specs=placed,
        out_specs=P(("grp", "wid"), "rep", "seq"),
        check_vma=False,
    )
```

```python
import functools

import jax
import jax.numpy as jnp
from jax import lax
from jax.experimental import pallas as pl
from jax.experimental.pallas import tpu as pltpu
from jax.sharding import PartitionSpec as P

BLK = 128
LEN = 64
MXU = 256
PIECES = 8
NT = (((1,), (1,)), ((), ()))
F32 = jnp.float32
BF16 = jnp.bfloat16
VMEM = pl.BlockSpec(memory_space=pltpu.VMEM)
HBM = pl.BlockSpec(memory_space=pltpu.HBM)
PARAMS = pltpu.CompilerParams(vmem_limit_bytes=16 << 20)


def two_parts(x):
    high = x.astype(BF16)
    return high, (x - high.astype(F32)).astype(BF16)


def product(left, right, dims):
    left_high, left_low = two_parts(left)
    right_high, right_low = two_parts(right)
    dot = functools.partial(lax.dot_general, dimension_numbers=dims, preferred_element_type=F32)
    return dot(left_high, right_high) + (dot(left_high, right_low) + dot(left_low, right_high))


def scaled_rows(rows, scale):
    return rows * jnp.concatenate([scale] * (rows.shape[0] // scale.shape[0]), axis=0)


def project_side(picked, scale_of, weights, side):
    _, chosen, pairs, _, _ = picked.shape
    tokens = jnp.concatenate(
        [
            jnp.concatenate(
                [scaled_rows(picked[side, block, pair], scale_of(block, pair)) for pair in range(pairs)],
                axis=0,
            )
            for block in range(chosen)
        ],
        axis=1,
    )
    factor = jnp.concatenate([weights[side, block] for block in range(chosen)], axis=1)
    return lax.dot_general(factor, tokens, NT, preferred_element_type=F32)


def project_other_kernel(
    act_index,
    grad_index,
    act_exponents,
    grad_exponents,
    act_blocks,
    grad_blocks,
    acts,
    grads,
    sent,
    picked_own,
    scales_own,
    weights,
    index,
    exponents,
    picked_other,
    small_sems,
    sems,
):
    own = lax.axis_index("rep")
    other = 1 - own
    _, chosen, pairs, _, _ = picked_own.shape
    block_count = exponents.shape[2]
    values = (acts, grads)
    small = []
    for place, (sources, target) in enumerate(
        (
            ((act_index, grad_index), index),
            ((act_exponents, grad_exponents), exponents),
            ((act_blocks, grad_blocks), weights),
        )
    ):
        for side, source in enumerate(sources):
            copy = pltpu.make_async_copy(source, target.at[side], small_sems.at[place, side])
            copy.start()
            small.append(copy)
    local = []
    for side in range(2):
        small[side].wait()
        local.append([lax.rem(index[side, block], block_count) for block in range(chosen)])
    copies = {}
    for place, (parity, target) in enumerate(((other, picked_other), (own, picked_own))):
        for side in range(2):
            for block in range(chosen):
                columns = pl.ds(pl.multiple_of(local[side][block] * BLK, BLK), BLK)
                copy = pltpu.make_async_copy(
                    values[side].at[:, parity, :, columns],
                    target.at[side, block],
                    sems.at[place, side, block],
                )
                copy.start()
                copies[place, side, block] = copy
    for copy in small[2:]:
        copy.wait()

    def scale_of(side, block, pair, parity):
        exponent = exponents[side, 2 * pair + parity, local[side][block]]
        return jnp.exp2(jnp.full((16, BLK), exponent, jnp.int32).astype(F32)).astype(BF16)

    for side in range(2):
        for block in range(chosen):
            for pair in range(pairs):
                scales_own[side, block, pair] = scale_of(side, block, pair, own)
    width = weights.shape[2]
    for side in range(2):
        for block in range(chosen):
            copies[0, side, block].wait()
        sent[side * width : (side + 1) * width, :] = project_side(
            picked_other, lambda block, pair: scale_of(side, block, pair, other), weights, side
        )
    for side in range(2):
        for block in range(chosen):
            copies[1, side, block].wait()


def project_other(indices, exponents, blocks, values):
    pairs, _, _, features = values[0].shape
    chosen, width, _ = blocks[0].shape
    tokens = pairs * LEN
    operands = [
        pltpu.with_memory_space_constraint(v, pltpu.HBM)
        for v in (*indices, *exponents, *blocks, *values)
    ]
    return pl.pallas_call(
        project_other_kernel,
        out_shape=(
            jax.ShapeDtypeStruct((2 * width, tokens), F32),
            jax.ShapeDtypeStruct((2, chosen, pairs, LEN, BLK), BF16),
            jax.ShapeDtypeStruct((2, chosen, pairs, 16, BLK), BF16),
            jax.ShapeDtypeStruct((2, chosen, width, BLK), BF16),
        ),
        in_specs=[HBM] * 8,
        out_specs=[VMEM] * 4,
        scratch_shapes=[
            pltpu.SMEM((2, chosen), jnp.int32),
            pltpu.SMEM((2, *exponents[0].shape), jnp.int32),
            pltpu.VMEM((2, chosen, pairs, LEN, BLK), BF16),
            pltpu.SemaphoreType.DMA((3, 2)),
            pltpu.SemaphoreType.DMA((2, 2, chosen)),
        ],
        cost_estimate=pl.CostEstimate(
            flops=4 * tokens * chosen * BLK * width,
            bytes_accessed=8 * tokens * chosen * BLK + 8 * tokens * width,
            transcendentals=0,
        ),
        compiler_params=PARAMS,
        name="project_other",
    )(*operands)


def project_own_kernel(picked, scales, weights, out):
    width = weights.shape[2]
    for side in range(2):
        out[side * width : (side + 1) * width, :] = project_side(
            picked, lambda block, pair: scales[side, block, pair], weights, side
        )


def project_own(picked, scales, weights):
    _, chosen, pairs, _, _ = picked.shape
    width = weights.shape[2]
    tokens = pairs * LEN
    return pl.pallas_call(
        project_own_kernel,
        out_shape=jax.ShapeDtypeStruct((2 * width, tokens), F32),
        in_specs=[VMEM] * 3,
        out_specs=VMEM,
        cost_estimate=pl.CostEstimate(
            flops=4 * tokens * chosen * BLK * width,
            bytes_accessed=4 * tokens * chosen * BLK + 8 * tokens * width,
            transcendentals=0,
        ),
        compiler_params=PARAMS,
        name="project_own",
    )(picked, scales, weights)


def split_pieces(fisher, high, low, held, sems):
    pieces, rows, _ = held.shape
    copies = [
        pltpu.make_async_copy(fisher.at[pl.ds(piece * rows, rows)], held.at[piece], sems.at[piece])
        for piece in range(pieces)
    ]
    for copy in copies:
        copy.start()
    for piece in range(pieces):
        copies[piece].wait()

        @pl.loop(0, rows // 16)
        def _(step):
            part_high, part_low = two_parts(held[piece, pl.ds(step * 16, 16), :])
            target = pl.ds(piece * rows + step * 16, 16)
            high[target, :] = part_high
            low[target, :] = part_low


def split_early_kernel(fisher, high, low, held, sems):
    @pl.when(lax.axis_index("rep") == 1)
    def _():
        split_pieces(fisher, high, low, held, sems)


def split_late_kernel(fisher, high_in, low_in, high, low, held, sems):
    first_core = lax.axis_index("rep") == 0

    @pl.when(first_core)
    def _():
        split_pieces(fisher, high, low, held, sems)

    @pl.when(~first_core)
    def _():
        @pl.loop(0, high.shape[0] // 16)
        def _(step):
            rows = pl.ds(pl.multiple_of(step * 16, 16), 16)
            high[rows, :] = high_in[rows, :]
            low[rows, :] = low_in[rows, :]


def split_fisher(fisher, *halves):
    rows, columns = fisher.shape
    half = jax.ShapeDtypeStruct((rows, columns), BF16)
    return pl.pallas_call(
        split_late_kernel if halves else split_early_kernel,
        out_shape=(half, half),
        in_specs=[HBM] + [VMEM] * len(halves),
        out_specs=(VMEM, VMEM),
        scratch_shapes=[
            pltpu.VMEM((PIECES, rows // PIECES, columns), F32),
            pltpu.SemaphoreType.DMA((PIECES,)),
        ],
        cost_estimate=pl.CostEstimate(
            flops=2 * rows * columns, bytes_accessed=8 * rows * columns, transcendentals=0
        ),
        compiler_params=PARAMS,
        name="split_late" if halves else "split_early",
    )(pltpu.with_memory_space_constraint(fisher, pltpu.HBM), *halves)


def message_kernel(width, own, other, *messages):
    wid = lax.axis_index("wid")
    count = len(messages) + 1
    share = width // count
    acts = own[:width, :] + other[:width, :]
    for shift, message in enumerate(messages, 1):
        target = lax.rem(wid + shift, count)
        rows = pl.ds(pl.multiple_of(width + target * share, share), share)
        message[:width, :] = acts
        message[width:, :] = own[rows, :] + other[rows, :]


def make_messages(own, other, wid_count):
    width = own.shape[0] // 2
    shape = jax.ShapeDtypeStruct((width + width // wid_count, own.shape[1]), F32)
    return pl.pallas_call(
        functools.partial(message_kernel, width),
        out_shape=[shape] * (wid_count - 1),
        in_specs=[VMEM] * 2,
        out_specs=[VMEM] * (wid_count - 1),
        compiler_params=PARAMS,
        name="make_messages",
    )(own, other)


def outer_kernel(width, own, other, *rest):
    *messages, out, staged = rest
    wid = lax.axis_index("wid")
    share = width // (len(messages) + 1)
    rows = pl.ds(pl.multiple_of(width + wid * share, share), share)
    acts = own[:width, :] + other[:width, :]
    grads = own[rows, :] + other[rows, :]
    for message in messages:
        acts = acts + message[:width, :]
        grads = grads + message[width:, :]
    half = share // 2
    pairs = acts.shape[1] // BLK
    lane = lax.broadcasted_iota(jnp.int32, (half, BLK), 1)
    for pair in range(pairs):
        columns = slice(pair * BLK, (pair + 1) * BLK)
        staged[pair] = grads[:, columns]
        pieces = []
        for odd in range(2):
            part = staged[pair, pl.ds(odd, half, stride=2), :]
            pieces.append(jnp.where(lane < LEN, part, 0.0))
            pieces.append(jnp.where(lane < LEN, 0.0, part))
        left = jnp.concatenate(pieces, axis=0)
        result = product(left, acts[:, columns], NT) * (1.0 / LEN)
        both = jnp.concatenate([result[: 2 * half, :], result[2 * half :, :]], axis=1)
        out[pl.ds(2 * pair, half, stride=2 * pairs), :] = both[:half, :]
        out[pl.ds(2 * pair + 1, half, stride=2 * pairs), :] = both[half:, :]


def outer_products(own, other, messages):
    width = own.shape[0] // 2
    tokens = own.shape[1]
    share = width // (len(messages) + 1)
    sequences = tokens // LEN
    return pl.pallas_call(
        functools.partial(outer_kernel, width),
        out_shape=jax.ShapeDtypeStruct((share // 2 * sequences, 2 * width), F32),
        in_specs=[VMEM] * (2 + len(messages)),
        out_specs=VMEM,
        scratch_shapes=[pltpu.VMEM((tokens // BLK, share, BLK), F32)],
        compiler_params=PARAMS,
        name="outer_products",
    )(own, other, *messages)


def tile_products(left_high, left_low, high, low):
    rows, columns = high.shape
    streamed = rows // 4 // MXU * MXU
    count = left_high.shape[0]
    both = jnp.concatenate([left_high, left_low], axis=0)
    dot = functools.partial(lax.dot_general, dimension_numbers=NT, preferred_element_type=F32)
    sums = None
    for start in range(0, columns, MXU):
        piece = slice(start, start + MXU)
        terms = []
        if streamed:
            terms.append(dot(high[:streamed, piece], both[:, piece]))
        terms.append(dot(both[:, piece], high[streamed:, piece]))
        if streamed:
            terms.append(dot(low[:streamed, piece], left_high[:, piece]))
        terms.append(dot(left_high[:, piece], low[streamed:, piece]))
        sums = terms if sums is None else [a + b for a, b in zip(sums, terms)]
    held_high, held_low = sums[1::2] if streamed else sums
    result = held_high[:count] + (held_high[count:] + held_low)
    if streamed:
        tall = sums[0][:, :count] + (sums[0][:, count:] + sums[2])
        result = jnp.concatenate([tall.T, result], axis=1)
    return result


def exchange_steps(seq_count):
    steps = range(1, seq_count)
    return list(zip(steps, sorted(steps, key=lambda step: (step.bit_count(), -step))))


def fisher_kernel(wid_count, *refs):
    seq_count = len(refs) - 3 - wid_count
    gathered = refs[:seq_count]
    high, low = refs[seq_count : seq_count + 2]
    outs = refs[seq_count + 2 : seq_count + 2 + wid_count]
    placed = refs[-1]
    seq = lax.axis_index("seq")
    wid = lax.axis_index("wid")
    per_wid = seq_count // wid_count
    sequences = placed.shape[2]
    steps = gathered[0].shape[0] // sequences
    rows = []
    for ref in gathered:
        rows.append(
            jnp.concatenate(
                [ref[step * sequences : (step + 1) * sequences, :] for step in range(steps)], axis=1
            )
        )
    left_high, left_low = two_parts(jnp.concatenate(rows, axis=0))
    result = tile_products(left_high, left_low, high, low)
    rep = lax.axis_index("rep")
    for shift, (first, second) in enumerate([(0, 0)] + exchange_steps(seq_count)):
        group = seq ^ jnp.where(rep == 0, first, second)
        target = lax.rem(group // per_wid - wid + wid_count, wid_count)
        placed[target, lax.rem(group, per_wid)] = result[shift * sequences : (shift + 1) * sequences]
    for target, out in enumerate(outs):
        for group in range(per_wid):
            out[group * sequences : (group + 1) * sequences, 0, :] = placed[target, group]


def fisher_product(gathered, high, low, wid_count):
    seq_count = len(gathered)
    rows, columns = high.shape
    sequences = gathered[0].shape[0] * BLK // columns
    per_wid = seq_count // wid_count
    shape = jax.ShapeDtypeStruct((per_wid * sequences, 1, rows), F32)
    return pl.pallas_call(
        functools.partial(fisher_kernel, wid_count),
        out_shape=[shape] * wid_count,
        in_specs=[VMEM] * (seq_count + 2),
        out_specs=[VMEM] * wid_count,
        scratch_shapes=[pltpu.VMEM((wid_count, per_wid, sequences, rows), F32)],
        compiler_params=PARAMS,
        name="fisher_product",
    )(*gathered, high, low)


def shifted(value, axis, shift):
    count = lax.axis_size(axis)
    return lax.ppermute(value, axis, [(i, (i + shift) % count) for i in range(count)])


def exchanged(value, steps):
    cores = lax.axis_size("rep")
    pairs = [
        (seq * cores + core, (seq ^ steps[core]) * cores + core)
        for seq in range(lax.axis_size("seq"))
        for core in range(cores)
    ]
    return lax.ppermute(value, ("seq", "rep"), pairs)


def shards(
    activations,
    output_grads,
    act_exponents,
    grad_exponents,
    input_blocks,
    input_index,
    output_blocks,
    output_index,
    fisher_inverse,
):
    seq_count = lax.axis_size("seq")
    wid_count = lax.axis_size("wid")
    pairs = activations.shape[0] // LEN // 2
    indices = (input_index, output_index)
    exponents = (act_exponents, grad_exponents)
    blocks = (jnp.swapaxes(input_blocks, 1, 2), jnp.swapaxes(output_blocks, 1, 2))
    values = tuple(v.reshape(pairs, 2, LEN, v.shape[1]) for v in (activations, output_grads))
    sent, *held = project_other(indices, exponents, blocks, values)
    other = shifted(sent, "rep", 1)
    own = project_own(*held)
    fisher, own = lax.optimization_barrier((fisher_inverse, own))
    halves = split_fisher(fisher)
    own, other, *halves = lax.optimization_barrier((own, other, *halves))
    messages = make_messages(own, other, wid_count)
    fisher, *messages = lax.optimization_barrier((fisher, *messages))
    received = [shifted(m, "wid", shift) for shift, m in enumerate(messages, 1)]
    high, low = split_fisher(fisher, *halves)
    own, high, low = lax.optimization_barrier((own, high, low))
    outer = outer_products(own, other, received)
    gathered = [outer] + [exchanged(outer, steps) for steps in exchange_steps(seq_count)]
    parts = fisher_product(gathered, high, low, wid_count)
    result = parts[0]
    for shift in range(1, wid_count):
        result = result + shifted(parts[shift], "wid", shift)
    return result


def solution(mesh):
    placed = (
        P(("grp", "seq"), ("wid", "rep")),
        P(("grp", "seq"), ("wid", "rep")),
        P(("grp", "seq"), ("wid", "rep")),
        P(("grp", "seq"), ("wid", "rep")),
        P(("wid", "rep"), None, None),
        P(("wid", "rep")),
        P(("wid", "rep"), None, None),
        P(("wid", "rep")),
        P("seq", "wid"),
    )
    return jax.shard_map(
        shards,
        mesh=mesh,
        in_specs=placed,
        out_specs=P(("grp", "wid"), "rep", "seq"),
        check_vma=False,
    )
```

```python
import functools

import jax
import jax.numpy as jnp
from jax import lax
from jax.experimental import pallas as pl
from jax.experimental.pallas import tpu as pltpu
from jax.sharding import PartitionSpec as P

BLK = 128
LEN = 64
MXU = 256
PIECES = 8
NT = (((1,), (1,)), ((), ()))
F32 = jnp.float32
BF16 = jnp.bfloat16
VMEM = pl.BlockSpec(memory_space=pltpu.VMEM)
HBM = pl.BlockSpec(memory_space=pltpu.HBM)
PARAMS = pltpu.CompilerParams(vmem_limit_bytes=16 << 20)


def two_parts(x):
    high = x.astype(BF16)
    return high, (x - high.astype(F32)).astype(BF16)


def product(left, right, dims):
    left_high, left_low = two_parts(left)
    right_high, right_low = two_parts(right)
    dot = functools.partial(lax.dot_general, dimension_numbers=dims, preferred_element_type=F32)
    rows = left.shape[0]
    main = dot(jnp.concatenate([left_high, left_low], axis=0), right_high)
    return main[:rows] + (main[rows:] + dot(left_high, right_low))


def scaled_rows(rows, scale):
    return rows * jnp.concatenate([scale] * (rows.shape[0] // scale.shape[0]), axis=0)


def project_side(picked, scale_of, weights, side):
    _, chosen, pairs, _, _ = picked.shape
    tokens = jnp.concatenate(
        [
            jnp.concatenate(
                [scaled_rows(picked[side, block, pair], scale_of(block, pair)) for pair in range(pairs)],
                axis=0,
            )
            for block in range(chosen)
        ],
        axis=1,
    )
    factor = jnp.concatenate([weights[side, block] for block in range(chosen)], axis=1)
    return lax.dot_general(factor, tokens, NT, preferred_element_type=F32)


def project_other_kernel(
    act_index,
    grad_index,
    act_exponents,
    grad_exponents,
    act_blocks,
    grad_blocks,
    acts,
    grads,
    sent,
    picked_own,
    scales_own,
    weights,
    index,
    exponents,
    picked_other,
    small_sems,
    sems,
):
    own = lax.axis_index("rep")
    other = 1 - own
    _, chosen, pairs, _, _ = picked_own.shape
    block_count = exponents.shape[2]
    values = (acts, grads)
    small = []
    for place, (sources, target) in enumerate(
        (
            ((act_index, grad_index), index),
            ((act_exponents, grad_exponents), exponents),
            ((act_blocks, grad_blocks), weights),
        )
    ):
        for side, source in enumerate(sources):
            copy = pltpu.make_async_copy(source, target.at[side], small_sems.at[place, side])
            copy.start()
            small.append(copy)
    local = []
    for side in range(2):
        small[side].wait()
        local.append([lax.rem(index[side, block], block_count) for block in range(chosen)])
    copies = {}
    for place, (parity, target) in enumerate(((other, picked_other), (own, picked_own))):
        for side in range(2):
            for block in range(chosen):
                columns = pl.ds(pl.multiple_of(local[side][block] * BLK, BLK), BLK)
                copy = pltpu.make_async_copy(
                    values[side].at[:, parity, :, columns],
                    target.at[side, block],
                    sems.at[place, side, block],
                )
                copy.start()
                copies[place, side, block] = copy
    for copy in small[2:]:
        copy.wait()

    def scale_of(side, block, pair, parity):
        exponent = exponents[side, 2 * pair + parity, local[side][block]]
        return jnp.exp2(jnp.full((16, BLK), exponent, jnp.int32).astype(F32)).astype(BF16)

    for side in range(2):
        for block in range(chosen):
            for pair in range(pairs):
                scales_own[side, block, pair] = scale_of(side, block, pair, own)
    width = weights.shape[2]
    for side in range(2):
        for block in range(chosen):
            copies[0, side, block].wait()
        sent[side * width : (side + 1) * width, :] = project_side(
            picked_other, lambda block, pair: scale_of(side, block, pair, other), weights, side
        )
    for side in range(2):
        for block in range(chosen):
            copies[1, side, block].wait()


def project_other(indices, exponents, blocks, values):
    pairs, _, _, features = values[0].shape
    chosen, width, _ = blocks[0].shape
    tokens = pairs * LEN
    operands = [
        pltpu.with_memory_space_constraint(v, pltpu.HBM)
        for v in (*indices, *exponents, *blocks, *values)
    ]
    return pl.pallas_call(
        project_other_kernel,
        out_shape=(
            jax.ShapeDtypeStruct((2 * width, tokens), F32),
            jax.ShapeDtypeStruct((2, chosen, pairs, LEN, BLK), BF16),
            jax.ShapeDtypeStruct((2, chosen, pairs, 16, BLK), BF16),
            jax.ShapeDtypeStruct((2, chosen, width, BLK), BF16),
        ),
        in_specs=[HBM] * 8,
        out_specs=[VMEM] * 4,
        scratch_shapes=[
            pltpu.SMEM((2, chosen), jnp.int32),
            pltpu.SMEM((2, *exponents[0].shape), jnp.int32),
            pltpu.VMEM((2, chosen, pairs, LEN, BLK), BF16),
            pltpu.SemaphoreType.DMA((3, 2)),
            pltpu.SemaphoreType.DMA((2, 2, chosen)),
        ],
        cost_estimate=pl.CostEstimate(
            flops=4 * tokens * chosen * BLK * width,
            bytes_accessed=8 * tokens * chosen * BLK + 8 * tokens * width,
            transcendentals=0,
        ),
        compiler_params=PARAMS,
        name="project_other",
    )(*operands)


def project_own_kernel(picked, scales, weights, out):
    width = weights.shape[2]
    for side in range(2):
        out[side * width : (side + 1) * width, :] = project_side(
            picked, lambda block, pair: scales[side, block, pair], weights, side
        )


def project_own(picked, scales, weights):
    _, chosen, pairs, _, _ = picked.shape
    width = weights.shape[2]
    tokens = pairs * LEN
    return pl.pallas_call(
        project_own_kernel,
        out_shape=jax.ShapeDtypeStruct((2 * width, tokens), F32),
        in_specs=[VMEM] * 3,
        out_specs=VMEM,
        cost_estimate=pl.CostEstimate(
            flops=4 * tokens * chosen * BLK * width,
            bytes_accessed=4 * tokens * chosen * BLK + 8 * tokens * width,
            transcendentals=0,
        ),
        compiler_params=PARAMS,
        name="project_own",
    )(picked, scales, weights)


def split_pieces(fisher, high, low, held, sems):
    pieces, rows, _ = held.shape
    copies = [
        pltpu.make_async_copy(fisher.at[pl.ds(piece * rows, rows)], held.at[piece], sems.at[piece])
        for piece in range(pieces)
    ]
    for copy in copies:
        copy.start()
    for piece in range(pieces):
        copies[piece].wait()

        @pl.loop(0, rows // 16)
        def _(step):
            part_high, part_low = two_parts(held[piece, pl.ds(step * 16, 16), :])
            target = pl.ds(piece * rows + step * 16, 16)
            high[target, :] = part_high
            low[target, :] = part_low


def split_early_kernel(fisher, high, low, held, sems):
    @pl.when(lax.axis_index("rep") == 1)
    def _():
        split_pieces(fisher, high, low, held, sems)


def split_late_kernel(fisher, high_in, low_in, high, low, held, sems):
    first_core = lax.axis_index("rep") == 0

    @pl.when(first_core)
    def _():
        split_pieces(fisher, high, low, held, sems)

    @pl.when(~first_core)
    def _():
        @pl.loop(0, high.shape[0] // 16)
        def _(step):
            rows = pl.ds(pl.multiple_of(step * 16, 16), 16)
            high[rows, :] = high_in[rows, :]
            low[rows, :] = low_in[rows, :]


def split_fisher(fisher, *halves):
    rows, columns = fisher.shape
    half = jax.ShapeDtypeStruct((rows, columns), BF16)
    return pl.pallas_call(
        split_late_kernel if halves else split_early_kernel,
        out_shape=(half, half),
        in_specs=[HBM] + [VMEM] * len(halves),
        out_specs=(VMEM, VMEM),
        scratch_shapes=[
            pltpu.VMEM((PIECES, rows // PIECES, columns), F32),
            pltpu.SemaphoreType.DMA((PIECES,)),
        ],
        cost_estimate=pl.CostEstimate(
            flops=2 * rows * columns, bytes_accessed=8 * rows * columns, transcendentals=0
        ),
        compiler_params=PARAMS,
        name="split_late" if halves else "split_early",
    )(pltpu.with_memory_space_constraint(fisher, pltpu.HBM), *halves)


def message_kernel(width, own, other, *messages):
    wid = lax.axis_index("wid")
    count = len(messages) + 1
    share = width // count
    acts = own[:width, :] + other[:width, :]
    for shift, message in enumerate(messages, 1):
        target = lax.rem(wid + shift, count)
        rows = pl.ds(pl.multiple_of(width + target * share, share), share)
        message[:width, :] = acts
        message[width:, :] = own[rows, :] + other[rows, :]


def make_messages(own, other, wid_count):
    width = own.shape[0] // 2
    shape = jax.ShapeDtypeStruct((width + width // wid_count, own.shape[1]), F32)
    return pl.pallas_call(
        functools.partial(message_kernel, width),
        out_shape=[shape] * (wid_count - 1),
        in_specs=[VMEM] * 2,
        out_specs=[VMEM] * (wid_count - 1),
        compiler_params=PARAMS,
        name="make_messages",
    )(own, other)


def outer_kernel(width, own, other, *rest):
    *messages, out, staged = rest
    wid = lax.axis_index("wid")
    share = width // (len(messages) + 1)
    rows = pl.ds(pl.multiple_of(width + wid * share, share), share)
    acts = own[:width, :] + other[:width, :]
    grads = own[rows, :] + other[rows, :]
    for message in messages:
        acts = acts + message[:width, :]
        grads = grads + message[width:, :]
    half = share // 2
    pairs = acts.shape[1] // BLK
    lane = lax.broadcasted_iota(jnp.int32, (half, BLK), 1)
    for pair in range(pairs):
        staged[pair] = grads[:, pair * BLK : (pair + 1) * BLK]
    results = []
    for pair in range(pairs):
        pieces = []
        for odd in range(2):
            part = staged[pair, pl.ds(odd, half, stride=2), :]
            pieces.append(jnp.where(lane < LEN, part, 0.0))
            pieces.append(jnp.where(lane < LEN, 0.0, part))
        left = jnp.concatenate(pieces, axis=0)
        results.append(product(left, acts[:, pair * BLK : (pair + 1) * BLK], NT) * (1.0 / LEN))
    for pair, result in enumerate(results):
        both = jnp.concatenate([result[: 2 * half, :], result[2 * half :, :]], axis=1)
        out[pl.ds(2 * pair, half, stride=2 * pairs), :] = both[:half, :]
        out[pl.ds(2 * pair + 1, half, stride=2 * pairs), :] = both[half:, :]


def outer_products(own, other, messages):
    width = own.shape[0] // 2
    tokens = own.shape[1]
    share = width // (len(messages) + 1)
    sequences = tokens // LEN
    return pl.pallas_call(
        functools.partial(outer_kernel, width),
        out_shape=jax.ShapeDtypeStruct((share // 2 * sequences, 2 * width), F32),
        in_specs=[VMEM] * (2 + len(messages)),
        out_specs=VMEM,
        scratch_shapes=[pltpu.VMEM((tokens // BLK, share, BLK), F32)],
        compiler_params=PARAMS,
        name="outer_products",
    )(own, other, *messages)


def tile_products(left_high, left_low, high, low):
    rows, columns = high.shape
    streamed = rows // 4 // MXU * MXU
    count = left_high.shape[0]
    both = jnp.concatenate([left_high, left_low], axis=0)
    dot = functools.partial(lax.dot_general, dimension_numbers=NT, preferred_element_type=F32)
    sums = None
    for start in range(0, columns, MXU):
        piece = slice(start, start + MXU)
        terms = []
        if streamed:
            terms.append(dot(high[:streamed, piece], both[:, piece]))
        terms.append(dot(both[:, piece], high[streamed:, piece]))
        if streamed:
            terms.append(dot(low[:streamed, piece], left_high[:, piece]))
        terms.append(dot(left_high[:, piece], low[streamed:, piece]))
        sums = terms if sums is None else [a + b for a, b in zip(sums, terms)]
    held_high, held_low = sums[1::2] if streamed else sums
    result = held_high[:count] + (held_high[count:] + held_low)
    if streamed:
        tall = sums[0][:, :count] + (sums[0][:, count:] + sums[2])
        result = jnp.concatenate([tall.T, result], axis=1)
    return result


def exchange_steps(seq_count):
    steps = range(1, seq_count)
    return list(zip(steps, sorted(steps, key=lambda step: (step.bit_count(), -step))))


def fisher_kernel(wid_count, *refs):
    seq_count = len(refs) - 3 - wid_count
    gathered = refs[:seq_count]
    high, low = refs[seq_count : seq_count + 2]
    outs = refs[seq_count + 2 : seq_count + 2 + wid_count]
    placed = refs[-1]
    seq = lax.axis_index("seq")
    wid = lax.axis_index("wid")
    per_wid = seq_count // wid_count
    sequences = placed.shape[2]
    steps = gathered[0].shape[0] // sequences
    rows = []
    for ref in gathered:
        rows.append(
            jnp.concatenate(
                [ref[step * sequences : (step + 1) * sequences, :] for step in range(steps)], axis=1
            )
        )
    left_high, left_low = two_parts(jnp.concatenate(rows, axis=0))
    result = tile_products(left_high, left_low, high, low)
    rep = lax.axis_index("rep")
    for shift, (first, second) in enumerate([(0, 0)] + exchange_steps(seq_count)):
        group = seq ^ jnp.where(rep == 0, first, second)
        target = lax.rem(group // per_wid - wid + wid_count, wid_count)
        placed[target, lax.rem(group, per_wid)] = result[shift * sequences : (shift + 1) * sequences]
    for target, out in enumerate(outs):
        for group in range(per_wid):
            out[group * sequences : (group + 1) * sequences, 0, :] = placed[target, group]


def fisher_product(gathered, high, low, wid_count):
    seq_count = len(gathered)
    rows, columns = high.shape
    sequences = gathered[0].shape[0] * BLK // columns
    per_wid = seq_count // wid_count
    shape = jax.ShapeDtypeStruct((per_wid * sequences, 1, rows), F32)
    return pl.pallas_call(
        functools.partial(fisher_kernel, wid_count),
        out_shape=[shape] * wid_count,
        in_specs=[VMEM] * (seq_count + 2),
        out_specs=[VMEM] * wid_count,
        scratch_shapes=[pltpu.VMEM((wid_count, per_wid, sequences, rows), F32)],
        compiler_params=PARAMS,
        name="fisher_product",
    )(*gathered, high, low)


def shifted(value, axis, shift):
    count = lax.axis_size(axis)
    return lax.ppermute(value, axis, [(i, (i + shift) % count) for i in range(count)])


def exchanged(value, steps):
    cores = lax.axis_size("rep")
    pairs = [
        (seq * cores + core, (seq ^ steps[core]) * cores + core)
        for seq in range(lax.axis_size("seq"))
        for core in range(cores)
    ]
    return lax.ppermute(value, ("seq", "rep"), pairs)


def shards(
    activations,
    output_grads,
    act_exponents,
    grad_exponents,
    input_blocks,
    input_index,
    output_blocks,
    output_index,
    fisher_inverse,
):
    seq_count = lax.axis_size("seq")
    wid_count = lax.axis_size("wid")
    pairs = activations.shape[0] // LEN // 2
    indices = (input_index, output_index)
    exponents = (act_exponents, grad_exponents)
    blocks = (jnp.swapaxes(input_blocks, 1, 2), jnp.swapaxes(output_blocks, 1, 2))
    values = tuple(v.reshape(pairs, 2, LEN, v.shape[1]) for v in (activations, output_grads))
    sent, *held = project_other(indices, exponents, blocks, values)
    other = shifted(sent, "rep", 1)
    own = project_own(*held)
    fisher, own = lax.optimization_barrier((fisher_inverse, own))
    halves = split_fisher(fisher)
    own, other, *halves = lax.optimization_barrier((own, other, *halves))
    messages = make_messages(own, other, wid_count)
    fisher, *messages = lax.optimization_barrier((fisher, *messages))
    received = [shifted(m, "wid", shift) for shift, m in enumerate(messages, 1)]
    high, low = split_fisher(fisher, *halves)
    own, high, low = lax.optimization_barrier((own, high, low))
    outer = outer_products(own, other, received)
    gathered = [outer] + [exchanged(outer, steps) for steps in exchange_steps(seq_count)]
    parts = fisher_product(gathered, high, low, wid_count)
    result = parts[0]
    for shift in range(1, wid_count):
        result = result + shifted(parts[shift], "wid", shift)
    return result


def solution(mesh):
    placed = (
        P(("grp", "seq"), ("wid", "rep")),
        P(("grp", "seq"), ("wid", "rep")),
        P(("grp", "seq"), ("wid", "rep")),
        P(("grp", "seq"), ("wid", "rep")),
        P(("wid", "rep"), None, None),
        P(("wid", "rep")),
        P(("wid", "rep"), None, None),
        P(("wid", "rep")),
        P("seq", "wid"),
    )
    return jax.shard_map(
        shards,
        mesh=mesh,
        in_specs=placed,
        out_specs=P(("grp", "wid"), "rep", "seq"),
        check_vma=False,
    )
```

```python
import functools

import jax
import jax.numpy as jnp
from jax import lax
from jax.experimental import pallas as pl
from jax.experimental.pallas import tpu as pltpu
from jax.sharding import PartitionSpec as P

BLK = 128
LEN = 64
MXU = 256
PIECES = 8
NT = (((1,), (1,)), ((), ()))
F32 = jnp.float32
BF16 = jnp.bfloat16
VMEM = pl.BlockSpec(memory_space=pltpu.VMEM)
HBM = pl.BlockSpec(memory_space=pltpu.HBM)
PARAMS = pltpu.CompilerParams(vmem_limit_bytes=16 << 20)


def two_parts(x):
    high = x.astype(BF16)
    return high, (x - high.astype(F32)).astype(BF16)


def product(left, right, dims):
    left_high, left_low = two_parts(left)
    right_high, right_low = two_parts(right)
    dot = functools.partial(lax.dot_general, dimension_numbers=dims, preferred_element_type=F32)
    rows = left.shape[0]
    main = dot(jnp.concatenate([left_high, left_low], axis=0), right_high)
    return main[:rows] + (main[rows:] + dot(left_high, right_low))


def scaled_rows(rows, scale):
    return rows * jnp.concatenate([scale] * (rows.shape[0] // scale.shape[0]), axis=0)


def project_side(picked, scale_of, weights, side):
    _, chosen, pairs, _, _ = picked.shape
    tokens = jnp.concatenate(
        [
            jnp.concatenate(
                [scaled_rows(picked[side, block, pair], scale_of(block, pair)) for pair in range(pairs)],
                axis=0,
            )
            for block in range(chosen)
        ],
        axis=1,
    )
    factor = jnp.concatenate([weights[side, block] for block in range(chosen)], axis=1)
    return lax.dot_general(factor, tokens, NT, preferred_element_type=F32)


def project_other_kernel(
    act_index,
    grad_index,
    act_exponents,
    grad_exponents,
    act_blocks,
    grad_blocks,
    acts,
    grads,
    sent,
    picked_own,
    scales_own,
    weights,
    index,
    exponents,
    picked_other,
    small_sems,
    sems,
):
    own = lax.axis_index("rep")
    other = 1 - own
    _, chosen, pairs, _, _ = picked_own.shape
    block_count = exponents.shape[2]
    values = (acts, grads)
    small = []
    for place, (sources, target) in enumerate(
        (
            ((act_index, grad_index), index),
            ((act_exponents, grad_exponents), exponents),
            ((act_blocks, grad_blocks), weights),
        )
    ):
        for side, source in enumerate(sources):
            copy = pltpu.make_async_copy(source, target.at[side], small_sems.at[place, side])
            copy.start()
            small.append(copy)
    local = []
    for side in range(2):
        small[side].wait()
        local.append([lax.rem(index[side, block], block_count) for block in range(chosen)])
    copies = {}
    for place, (parity, target) in enumerate(((other, picked_other), (own, picked_own))):
        for side in range(2):
            for block in range(chosen):
                columns = pl.ds(pl.multiple_of(local[side][block] * BLK, BLK), BLK)
                copy = pltpu.make_async_copy(
                    values[side].at[:, parity, :, columns],
                    target.at[side, block],
                    sems.at[place, side, block],
                )
                copy.start()
                copies[place, side, block] = copy
    for copy in small[2:]:
        copy.wait()

    def scale_of(side, block, pair, parity):
        exponent = exponents[side, 2 * pair + parity, local[side][block]]
        return jnp.exp2(jnp.full((16, BLK), exponent, jnp.int32).astype(F32)).astype(BF16)

    for side in range(2):
        for block in range(chosen):
            for pair in range(pairs):
                scales_own[side, block, pair] = scale_of(side, block, pair, own)
    width = weights.shape[2]
    for side in range(2):
        for block in range(chosen):
            copies[0, side, block].wait()
        sent[side * width : (side + 1) * width, :] = project_side(
            picked_other, lambda block, pair: scale_of(side, block, pair, other), weights, side
        )
    for side in range(2):
        for block in range(chosen):
            copies[1, side, block].wait()


def project_other(indices, exponents, blocks, values):
    pairs, _, _, features = values[0].shape
    chosen, width, _ = blocks[0].shape
    tokens = pairs * LEN
    operands = [
        pltpu.with_memory_space_constraint(v, pltpu.HBM)
        for v in (*indices, *exponents, *blocks, *values)
    ]
    return pl.pallas_call(
        project_other_kernel,
        out_shape=(
            jax.ShapeDtypeStruct((2 * width, tokens), F32),
            jax.ShapeDtypeStruct((2, chosen, pairs, LEN, BLK), BF16),
            jax.ShapeDtypeStruct((2, chosen, pairs, 16, BLK), BF16),
            jax.ShapeDtypeStruct((2, chosen, width, BLK), BF16),
        ),
        in_specs=[HBM] * 8,
        out_specs=[VMEM] * 4,
        scratch_shapes=[
            pltpu.SMEM((2, chosen), jnp.int32),
            pltpu.SMEM((2, *exponents[0].shape), jnp.int32),
            pltpu.VMEM((2, chosen, pairs, LEN, BLK), BF16),
            pltpu.SemaphoreType.DMA((3, 2)),
            pltpu.SemaphoreType.DMA((2, 2, chosen)),
        ],
        cost_estimate=pl.CostEstimate(
            flops=4 * tokens * chosen * BLK * width,
            bytes_accessed=8 * tokens * chosen * BLK + 8 * tokens * width,
            transcendentals=0,
        ),
        compiler_params=PARAMS,
        name="project_other",
    )(*operands)


def project_own_kernel(picked, scales, weights, out):
    width = weights.shape[2]
    for side in range(2):
        out[side * width : (side + 1) * width, :] = project_side(
            picked, lambda block, pair: scales[side, block, pair], weights, side
        )


def project_own(picked, scales, weights):
    _, chosen, pairs, _, _ = picked.shape
    width = weights.shape[2]
    tokens = pairs * LEN
    return pl.pallas_call(
        project_own_kernel,
        out_shape=jax.ShapeDtypeStruct((2 * width, tokens), F32),
        in_specs=[VMEM] * 3,
        out_specs=VMEM,
        cost_estimate=pl.CostEstimate(
            flops=4 * tokens * chosen * BLK * width,
            bytes_accessed=4 * tokens * chosen * BLK + 8 * tokens * width,
            transcendentals=0,
        ),
        compiler_params=PARAMS,
        name="project_own",
    )(picked, scales, weights)


def split_pieces(fisher, high, low, held, sems):
    pieces, rows, _ = held.shape
    copies = [
        pltpu.make_async_copy(fisher.at[pl.ds(piece * rows, rows)], held.at[piece], sems.at[piece])
        for piece in range(pieces)
    ]
    for copy in copies:
        copy.start()
    for piece in range(pieces):
        copies[piece].wait()

        @pl.loop(0, rows // 16)
        def _(step):
            part_high, part_low = two_parts(held[piece, pl.ds(step * 16, 16), :])
            target = pl.ds(piece * rows + step * 16, 16)
            high[target, :] = part_high
            low[target, :] = part_low


def split_early_kernel(fisher, high, low, held, sems):
    @pl.when(lax.axis_index("rep") == 1)
    def _():
        split_pieces(fisher, high, low, held, sems)


def split_late_kernel(fisher, high_in, low_in, high, low, held, sems):
    first_core = lax.axis_index("rep") == 0

    @pl.when(first_core)
    def _():
        split_pieces(fisher, high, low, held, sems)

    @pl.when(~first_core)
    def _():
        @pl.loop(0, high.shape[0] // 16)
        def _(step):
            rows = pl.ds(pl.multiple_of(step * 16, 16), 16)
            high[rows, :] = high_in[rows, :]
            low[rows, :] = low_in[rows, :]


def split_fisher(fisher, *halves):
    rows, columns = fisher.shape
    half = jax.ShapeDtypeStruct((rows, columns), BF16)
    return pl.pallas_call(
        split_late_kernel if halves else split_early_kernel,
        out_shape=(half, half),
        in_specs=[HBM] + [VMEM] * len(halves),
        out_specs=(VMEM, VMEM),
        scratch_shapes=[
            pltpu.VMEM((PIECES, rows // PIECES, columns), F32),
            pltpu.SemaphoreType.DMA((PIECES,)),
        ],
        cost_estimate=pl.CostEstimate(
            flops=2 * rows * columns, bytes_accessed=8 * rows * columns, transcendentals=0
        ),
        compiler_params=PARAMS,
        name="split_late" if halves else "split_early",
    )(pltpu.with_memory_space_constraint(fisher, pltpu.HBM), *halves)


def message_kernel(width, own, other, *messages):
    wid = lax.axis_index("wid")
    count = len(messages) + 1
    share = width // count
    acts = own[:width, :] + other[:width, :]
    for shift, message in enumerate(messages, 1):
        target = lax.rem(wid + shift, count)
        rows = pl.ds(pl.multiple_of(width + target * share, share), share)
        message[:width, :] = acts
        message[width:, :] = own[rows, :] + other[rows, :]


def make_messages(own, other, wid_count):
    width = own.shape[0] // 2
    shape = jax.ShapeDtypeStruct((width + width // wid_count, own.shape[1]), F32)
    return pl.pallas_call(
        functools.partial(message_kernel, width),
        out_shape=[shape] * (wid_count - 1),
        in_specs=[VMEM] * 2,
        out_specs=[VMEM] * (wid_count - 1),
        compiler_params=PARAMS,
        name="make_messages",
    )(own, other)


def outer_kernel(width, own, other, *rest):
    *messages, out, staged = rest
    wid = lax.axis_index("wid")
    share = width // (len(messages) + 1)
    rows = pl.ds(pl.multiple_of(width + wid * share, share), share)
    acts = own[:width, :] + other[:width, :]
    grads = own[rows, :] + other[rows, :]
    for message in messages:
        acts = acts + message[:width, :]
        grads = grads + message[width:, :]
    half = share // 2
    pairs = acts.shape[1] // BLK
    lane = lax.broadcasted_iota(jnp.int32, (half, BLK), 1)
    for pair in range(pairs):
        staged[pair] = grads[:, pair * BLK : (pair + 1) * BLK]
    results = []
    for pair in range(pairs):
        pieces = []
        for odd in range(2):
            part = staged[pair, pl.ds(odd, half, stride=2), :]
            pieces.append(jnp.where(lane < LEN, part, 0.0))
            pieces.append(jnp.where(lane < LEN, 0.0, part))
        left = jnp.concatenate(pieces, axis=0)
        results.append(product(left, acts[:, pair * BLK : (pair + 1) * BLK], NT) * (1.0 / LEN))
    for pair, result in enumerate(results):
        both = jnp.concatenate([result[: 2 * half, :], result[2 * half :, :]], axis=1)
        out[pl.ds(2 * pair, half, stride=2 * pairs), :] = both[:half, :]
        out[pl.ds(2 * pair + 1, half, stride=2 * pairs), :] = both[half:, :]


def outer_products(own, other, messages):
    width = own.shape[0] // 2
    tokens = own.shape[1]
    share = width // (len(messages) + 1)
    sequences = tokens // LEN
    return pl.pallas_call(
        functools.partial(outer_kernel, width),
        out_shape=jax.ShapeDtypeStruct((share // 2 * sequences, 2 * width), F32),
        in_specs=[VMEM] * (2 + len(messages)),
        out_specs=VMEM,
        scratch_shapes=[pltpu.VMEM((tokens // BLK, share, BLK), F32)],
        compiler_params=PARAMS,
        name="outer_products",
    )(own, other, *messages)


def tile_products(left_high, left_low, high, low):
    rows, columns = high.shape
    streamed = rows // 4 // MXU * MXU
    count = left_high.shape[0]
    both = jnp.concatenate([left_high, left_low], axis=0)
    dot = functools.partial(lax.dot_general, dimension_numbers=NT, preferred_element_type=F32)
    sums = None
    for start in range(0, columns, MXU):
        piece = slice(start, start + MXU)
        terms = []
        if streamed:
            terms.append(dot(high[:streamed, piece], both[:, piece]))
        terms.append(dot(both[:, piece], high[streamed:, piece]))
        if streamed:
            terms.append(dot(low[:streamed, piece], left_high[:, piece]))
        terms.append(dot(left_high[:, piece], low[streamed:, piece]))
        sums = terms if sums is None else [a + b for a, b in zip(sums, terms)]
    held_high, held_low = sums[1::2] if streamed else sums
    result = held_high[:count] + (held_high[count:] + held_low)
    if streamed:
        tall = sums[0][:, :count] + (sums[0][:, count:] + sums[2])
        result = jnp.concatenate([tall.T, result], axis=1)
    return result


def exchange_steps(seq_count):
    steps = range(1, seq_count)
    return list(zip(steps, sorted(steps, key=lambda step: (step.bit_count(), -step))))


def fisher_kernel(*refs):
    seq_count = len(refs) - 3
    wid_count, owned = refs[-1].shape[:2]
    gathered = refs[:seq_count]
    high, low = refs[seq_count : seq_count + 2]
    out = refs[-1]
    seq = lax.axis_index("seq")
    wid = lax.axis_index("wid")
    per_wid = seq_count // wid_count
    sequences = owned // per_wid
    steps = gathered[0].shape[0] // sequences
    rows = []
    for ref in gathered:
        rows.append(
            jnp.concatenate(
                [ref[step * sequences : (step + 1) * sequences, :] for step in range(steps)], axis=1
            )
        )
    left_high, left_low = two_parts(jnp.concatenate(rows, axis=0))
    result = tile_products(left_high, left_low, high, low)
    rep = lax.axis_index("rep")
    for shift, (first, second) in enumerate([(0, 0)] + exchange_steps(seq_count)):
        group = seq ^ jnp.where(rep == 0, first, second)
        target = lax.rem(group // per_wid - wid + wid_count, wid_count)
        rows = pl.ds(pl.multiple_of(lax.rem(group, per_wid) * sequences, sequences), sequences)
        out[target, rows, 0, :] = result[shift * sequences : (shift + 1) * sequences]


def fisher_product(gathered, high, low, wid_count):
    seq_count = len(gathered)
    rows, columns = high.shape
    sequences = gathered[0].shape[0] * BLK // columns
    per_wid = seq_count // wid_count
    return pl.pallas_call(
        fisher_kernel,
        out_shape=jax.ShapeDtypeStruct((wid_count, per_wid * sequences, 1, rows), F32),
        in_specs=[VMEM] * (seq_count + 2),
        out_specs=VMEM,
        compiler_params=PARAMS,
        name="fisher_product",
    )(*gathered, high, low)


def shifted(value, axis, shift):
    count = lax.axis_size(axis)
    return lax.ppermute(value, axis, [(i, (i + shift) % count) for i in range(count)])


def exchanged(value, steps):
    cores = lax.axis_size("rep")
    pairs = [
        (seq * cores + core, (seq ^ steps[core]) * cores + core)
        for seq in range(lax.axis_size("seq"))
        for core in range(cores)
    ]
    return lax.ppermute(value, ("seq", "rep"), pairs)


def shards(
    activations,
    output_grads,
    act_exponents,
    grad_exponents,
    input_blocks,
    input_index,
    output_blocks,
    output_index,
    fisher_inverse,
):
    seq_count = lax.axis_size("seq")
    wid_count = lax.axis_size("wid")
    pairs = activations.shape[0] // LEN // 2
    indices = (input_index, output_index)
    exponents = (act_exponents, grad_exponents)
    blocks = (jnp.swapaxes(input_blocks, 1, 2), jnp.swapaxes(output_blocks, 1, 2))
    values = tuple(v.reshape(pairs, 2, LEN, v.shape[1]) for v in (activations, output_grads))
    sent, *held = project_other(indices, exponents, blocks, values)
    other = shifted(sent, "rep", 1)
    own = project_own(*held)
    fisher, own = lax.optimization_barrier((fisher_inverse, own))
    halves = split_fisher(fisher)
    own, other, *halves = lax.optimization_barrier((own, other, *halves))
    messages = make_messages(own, other, wid_count)
    fisher, *messages = lax.optimization_barrier((fisher, *messages))
    received = [shifted(m, "wid", shift) for shift, m in enumerate(messages, 1)]
    high, low = split_fisher(fisher, *halves)
    own, high, low = lax.optimization_barrier((own, high, low))
    outer = outer_products(own, other, received)
    gathered = [outer] + [exchanged(outer, steps) for steps in exchange_steps(seq_count)]
    parts = fisher_product(gathered, high, low, wid_count)
    result = parts[0]
    for shift in range(1, wid_count):
        result = result + shifted(parts[shift], "wid", shift)
    return result


def solution(mesh):
    placed = (
        P(("grp", "seq"), ("wid", "rep")),
        P(("grp", "seq"), ("wid", "rep")),
        P(("grp", "seq"), ("wid", "rep")),
        P(("grp", "seq"), ("wid", "rep")),
        P(("wid", "rep"), None, None),
        P(("wid", "rep")),
        P(("wid", "rep"), None, None),
        P(("wid", "rep")),
        P("seq", "wid"),
    )
    return jax.shard_map(
        shards,
        mesh=mesh,
        in_specs=placed,
        out_specs=P(("grp", "wid"), "rep", "seq"),
        check_vma=False,
    )
```

```python
import functools

import jax
import jax.numpy as jnp
from jax import lax
from jax.experimental import pallas as pl
from jax.experimental.pallas import tpu as pltpu
from jax.sharding import PartitionSpec as P

BLK = 128
LEN = 64
MXU = 256
PIECES = 8
NT = (((1,), (1,)), ((), ()))
F32 = jnp.float32
BF16 = jnp.bfloat16
VMEM = pl.BlockSpec(memory_space=pltpu.VMEM)
HBM = pl.BlockSpec(memory_space=pltpu.HBM)
PARAMS = pltpu.CompilerParams(vmem_limit_bytes=16 << 20)


def two_parts(x):
    high = x.astype(BF16)
    return high, (x - high.astype(F32)).astype(BF16)


def product(left, right, dims):
    left_high, left_low = two_parts(left)
    right_high, right_low = two_parts(right)
    dot = functools.partial(lax.dot_general, dimension_numbers=dims, preferred_element_type=F32)
    rows = left.shape[0]
    main = dot(jnp.concatenate([left_high, left_low], axis=0), right_high)
    return main[:rows] + (main[rows:] + dot(left_high, right_low))


def scaled_rows(rows, scale):
    return rows * jnp.concatenate([scale] * (rows.shape[0] // scale.shape[0]), axis=0)


def project_side(picked, scale_of, weights, side):
    _, chosen, pairs, _, _ = picked.shape
    tokens = jnp.concatenate(
        [
            jnp.concatenate(
                [scaled_rows(picked[side, block, pair], scale_of(block, pair)) for pair in range(pairs)],
                axis=0,
            )
            for block in range(chosen)
        ],
        axis=1,
    )
    factor = jnp.concatenate([weights[side, block] for block in range(chosen)], axis=1)
    return lax.dot_general(factor, tokens, NT, preferred_element_type=F32)


def project_other_kernel(
    act_index,
    grad_index,
    act_exponents,
    grad_exponents,
    act_blocks,
    grad_blocks,
    acts,
    grads,
    sent,
    picked_own,
    scales_own,
    weights,
    index,
    exponents,
    picked_other,
    small_sems,
    sems,
):
    own = lax.axis_index("rep")
    other = 1 - own
    _, chosen, pairs, _, _ = picked_own.shape
    block_count = exponents.shape[2]
    values = (acts, grads)
    small = []
    for place, (sources, target) in enumerate(
        (
            ((act_index, grad_index), index),
            ((act_exponents, grad_exponents), exponents),
            ((act_blocks, grad_blocks), weights),
        )
    ):
        for side, source in enumerate(sources):
            copy = pltpu.make_async_copy(source, target.at[side], small_sems.at[place, side])
            copy.start()
            small.append(copy)
    local = []
    for side in range(2):
        small[side].wait()
        local.append([lax.rem(index[side, block], block_count) for block in range(chosen)])
    copies = {}
    for place, (parity, target) in enumerate(((other, picked_other), (own, picked_own))):
        for side in range(2):
            for block in range(chosen):
                columns = pl.ds(pl.multiple_of(local[side][block] * BLK, BLK), BLK)
                copy = pltpu.make_async_copy(
                    values[side].at[:, parity, :, columns],
                    target.at[side, block],
                    sems.at[place, side, block],
                )
                copy.start()
                copies[place, side, block] = copy
    for copy in small[2:]:
        copy.wait()

    def scale_of(side, block, pair, parity):
        exponent = exponents[side, 2 * pair + parity, local[side][block]]
        return jnp.exp2(jnp.full((16, BLK), exponent, jnp.int32).astype(F32)).astype(BF16)

    for side in range(2):
        for block in range(chosen):
            for pair in range(pairs):
                scales_own[side, block, pair] = scale_of(side, block, pair, own)
    width = weights.shape[2]
    for side in range(2):
        for block in range(chosen):
            copies[0, side, block].wait()
        sent[side * width : (side + 1) * width, :] = project_side(
            picked_other, lambda block, pair: scale_of(side, block, pair, other), weights, side
        )
    for side in range(2):
        for block in range(chosen):
            copies[1, side, block].wait()


def project_other(indices, exponents, blocks, values):
    pairs, _, _, features = values[0].shape
    chosen, width, _ = blocks[0].shape
    tokens = pairs * LEN
    operands = [
        pltpu.with_memory_space_constraint(v, pltpu.HBM)
        for v in (*indices, *exponents, *blocks, *values)
    ]
    return pl.pallas_call(
        project_other_kernel,
        out_shape=(
            jax.ShapeDtypeStruct((2 * width, tokens), F32),
            jax.ShapeDtypeStruct((2, chosen, pairs, LEN, BLK), BF16),
            jax.ShapeDtypeStruct((2, chosen, pairs, 16, BLK), BF16),
            jax.ShapeDtypeStruct((2, chosen, width, BLK), BF16),
        ),
        in_specs=[HBM] * 8,
        out_specs=[VMEM] * 4,
        scratch_shapes=[
            pltpu.SMEM((2, chosen), jnp.int32),
            pltpu.SMEM((2, *exponents[0].shape), jnp.int32),
            pltpu.VMEM((2, chosen, pairs, LEN, BLK), BF16),
            pltpu.SemaphoreType.DMA((3, 2)),
            pltpu.SemaphoreType.DMA((2, 2, chosen)),
        ],
        cost_estimate=pl.CostEstimate(
            flops=4 * tokens * chosen * BLK * width,
            bytes_accessed=8 * tokens * chosen * BLK + 8 * tokens * width,
            transcendentals=0,
        ),
        compiler_params=PARAMS,
        name="project_other",
    )(*operands)


def project_own_kernel(picked, scales, weights, out):
    width = weights.shape[2]
    for side in range(2):
        out[side * width : (side + 1) * width, :] = project_side(
            picked, lambda block, pair: scales[side, block, pair], weights, side
        )


def project_own(picked, scales, weights):
    _, chosen, pairs, _, _ = picked.shape
    width = weights.shape[2]
    tokens = pairs * LEN
    return pl.pallas_call(
        project_own_kernel,
        out_shape=jax.ShapeDtypeStruct((2 * width, tokens), F32),
        in_specs=[VMEM] * 3,
        out_specs=VMEM,
        cost_estimate=pl.CostEstimate(
            flops=4 * tokens * chosen * BLK * width,
            bytes_accessed=4 * tokens * chosen * BLK + 8 * tokens * width,
            transcendentals=0,
        ),
        compiler_params=PARAMS,
        name="project_own",
    )(picked, scales, weights)


def split_pieces(fisher, high, low, held, sems):
    pieces, rows, _ = held.shape
    copies = [
        pltpu.make_async_copy(fisher.at[pl.ds(piece * rows, rows)], held.at[piece], sems.at[piece])
        for piece in range(pieces)
    ]
    for copy in copies:
        copy.start()
    for piece in range(pieces):
        copies[piece].wait()

        @pl.loop(0, rows // 16)
        def _(step):
            part_high, part_low = two_parts(held[piece, pl.ds(step * 16, 16), :])
            target = pl.ds(piece * rows + step * 16, 16)
            high[target, :] = part_high
            low[target, :] = part_low


def split_early_kernel(fisher, high, low, held, sems):
    @pl.when(lax.axis_index("rep") == 1)
    def _():
        split_pieces(fisher, high, low, held, sems)


def split_late_kernel(fisher, high_in, low_in, high, low, held, sems):
    first_core = lax.axis_index("rep") == 0

    @pl.when(first_core)
    def _():
        split_pieces(fisher, high, low, held, sems)

    @pl.when(~first_core)
    def _():
        @pl.loop(0, high.shape[0] // 16)
        def _(step):
            rows = pl.ds(pl.multiple_of(step * 16, 16), 16)
            high[rows, :] = high_in[rows, :]
            low[rows, :] = low_in[rows, :]


def split_fisher(fisher, *halves):
    rows, columns = fisher.shape
    half = jax.ShapeDtypeStruct((rows, columns), BF16)
    return pl.pallas_call(
        split_late_kernel if halves else split_early_kernel,
        out_shape=(half, half),
        in_specs=[HBM] + [VMEM] * len(halves),
        out_specs=(VMEM, VMEM),
        scratch_shapes=[
            pltpu.VMEM((PIECES, rows // PIECES, columns), F32),
            pltpu.SemaphoreType.DMA((PIECES,)),
        ],
        cost_estimate=pl.CostEstimate(
            flops=2 * rows * columns, bytes_accessed=8 * rows * columns, transcendentals=0
        ),
        compiler_params=PARAMS,
        name="split_late" if halves else "split_early",
    )(pltpu.with_memory_space_constraint(fisher, pltpu.HBM), *halves)


def message_kernel(width, own, other, *messages):
    wid = lax.axis_index("wid")
    count = len(messages) + 1
    share = width // count
    acts = own[:width, :] + other[:width, :]
    for shift, message in enumerate(messages, 1):
        target = lax.rem(wid + shift, count)
        rows = pl.ds(pl.multiple_of(width + target * share, share), share)
        message[:width, :] = acts
        message[width:, :] = own[rows, :] + other[rows, :]


def make_messages(own, other, wid_count):
    width = own.shape[0] // 2
    shape = jax.ShapeDtypeStruct((width + width // wid_count, own.shape[1]), F32)
    return pl.pallas_call(
        functools.partial(message_kernel, width),
        out_shape=[shape] * (wid_count - 1),
        in_specs=[VMEM] * 2,
        out_specs=[VMEM] * (wid_count - 1),
        compiler_params=PARAMS,
        name="make_messages",
    )(own, other)


def outer_kernel(width, own, other, sent, *rest):
    *messages, out, staged = rest
    wid = lax.axis_index("wid")
    share = width // (len(messages) + 1)
    rows = pl.ds(pl.multiple_of(width + wid * share, share), share)
    acts = sent[:width, :]
    grads = own[rows, :] + other[rows, :]
    for message in messages:
        acts = acts + message[:width, :]
        grads = grads + message[width:, :]
    half = share // 2
    pairs = acts.shape[1] // BLK
    lane = lax.broadcasted_iota(jnp.int32, (half, BLK), 1)
    for pair in range(pairs):
        staged[pair] = grads[:, pair * BLK : (pair + 1) * BLK]
    results = []
    for pair in range(pairs):
        pieces = []
        for odd in range(2):
            part = staged[pair, pl.ds(odd, half, stride=2), :]
            pieces.append(jnp.where(lane < LEN, part, 0.0))
            pieces.append(jnp.where(lane < LEN, 0.0, part))
        left = jnp.concatenate(pieces, axis=0)
        results.append(product(left, acts[:, pair * BLK : (pair + 1) * BLK], NT) * (1.0 / LEN))
    for pair, result in enumerate(results):
        both = jnp.concatenate([result[: 2 * half, :], result[2 * half :, :]], axis=1)
        out[pl.ds(2 * pair, half, stride=2 * pairs), :] = both[:half, :]
        out[pl.ds(2 * pair + 1, half, stride=2 * pairs), :] = both[half:, :]


def outer_products(own, other, sent, messages):
    width = own.shape[0] // 2
    tokens = own.shape[1]
    share = width // (len(messages) + 1)
    sequences = tokens // LEN
    return pl.pallas_call(
        functools.partial(outer_kernel, width),
        out_shape=jax.ShapeDtypeStruct((share // 2 * sequences, 2 * width), F32),
        in_specs=[VMEM] * (3 + len(messages)),
        out_specs=VMEM,
        scratch_shapes=[pltpu.VMEM((tokens // BLK, share, BLK), F32)],
        compiler_params=PARAMS,
        name="outer_products",
    )(own, other, sent, *messages)


def tile_products(left_high, left_low, high, low):
    rows, columns = high.shape
    streamed = rows // 4 // MXU * MXU
    count = left_high.shape[0]
    both = jnp.concatenate([left_high, left_low], axis=0)
    dot = functools.partial(lax.dot_general, dimension_numbers=NT, preferred_element_type=F32)
    sums = None
    for start in range(0, columns, MXU):
        piece = slice(start, start + MXU)
        terms = []
        if streamed:
            terms.append(dot(high[:streamed, piece], both[:, piece]))
        terms.append(dot(both[:, piece], high[streamed:, piece]))
        if streamed:
            terms.append(dot(low[:streamed, piece], left_high[:, piece]))
        terms.append(dot(left_high[:, piece], low[streamed:, piece]))
        sums = terms if sums is None else [a + b for a, b in zip(sums, terms)]
    held_high, held_low = sums[1::2] if streamed else sums
    result = held_high[:count] + (held_high[count:] + held_low)
    if streamed:
        tall = sums[0][:, :count] + (sums[0][:, count:] + sums[2])
        result = jnp.concatenate([tall.T, result], axis=1)
    return result


def exchange_steps(seq_count):
    steps = range(1, seq_count)
    return list(zip(steps, sorted(steps, key=lambda step: (step.bit_count(), -step))))


def fisher_kernel(*refs):
    seq_count = len(refs) - 3
    wid_count, owned = refs[-1].shape[:2]
    gathered = refs[:seq_count]
    high, low = refs[seq_count : seq_count + 2]
    out = refs[-1]
    seq = lax.axis_index("seq")
    wid = lax.axis_index("wid")
    per_wid = seq_count // wid_count
    sequences = owned // per_wid
    steps = gathered[0].shape[0] // sequences
    rows = []
    for ref in gathered:
        rows.append(
            jnp.concatenate(
                [ref[step * sequences : (step + 1) * sequences, :] for step in range(steps)], axis=1
            )
        )
    left_high, left_low = two_parts(jnp.concatenate(rows, axis=0))
    result = tile_products(left_high, left_low, high, low)
    rep = lax.axis_index("rep")
    for shift, (first, second) in enumerate([(0, 0)] + exchange_steps(seq_count)):
        group = seq ^ jnp.where(rep == 0, first, second)
        target = lax.rem(group // per_wid - wid + wid_count, wid_count)
        rows = pl.ds(pl.multiple_of(lax.rem(group, per_wid) * sequences, sequences), sequences)
        out[target, rows, 0, :] = result[shift * sequences : (shift + 1) * sequences]


def fisher_product(gathered, high, low, wid_count):
    seq_count = len(gathered)
    rows, columns = high.shape
    sequences = gathered[0].shape[0] * BLK // columns
    per_wid = seq_count // wid_count
    return pl.pallas_call(
        fisher_kernel,
        out_shape=jax.ShapeDtypeStruct((wid_count, per_wid * sequences, 1, rows), F32),
        in_specs=[VMEM] * (seq_count + 2),
        out_specs=VMEM,
        compiler_params=PARAMS,
        name="fisher_product",
    )(*gathered, high, low)


def shifted(value, axis, shift):
    count = lax.axis_size(axis)
    return lax.ppermute(value, axis, [(i, (i + shift) % count) for i in range(count)])


def exchanged(value, steps):
    cores = lax.axis_size("rep")
    pairs = [
        (seq * cores + core, (seq ^ steps[core]) * cores + core)
        for seq in range(lax.axis_size("seq"))
        for core in range(cores)
    ]
    return lax.ppermute(value, ("seq", "rep"), pairs)


def shards(
    activations,
    output_grads,
    act_exponents,
    grad_exponents,
    input_blocks,
    input_index,
    output_blocks,
    output_index,
    fisher_inverse,
):
    seq_count = lax.axis_size("seq")
    wid_count = lax.axis_size("wid")
    pairs = activations.shape[0] // LEN // 2
    indices = (input_index, output_index)
    exponents = (act_exponents, grad_exponents)
    blocks = (jnp.swapaxes(input_blocks, 1, 2), jnp.swapaxes(output_blocks, 1, 2))
    values = tuple(v.reshape(pairs, 2, LEN, v.shape[1]) for v in (activations, output_grads))
    sent, *held = project_other(indices, exponents, blocks, values)
    other = shifted(sent, "rep", 1)
    own = project_own(*held)
    fisher, own = lax.optimization_barrier((fisher_inverse, own))
    halves = split_fisher(fisher)
    own, other, *halves = lax.optimization_barrier((own, other, *halves))
    messages = make_messages(own, other, wid_count)
    fisher, *messages = lax.optimization_barrier((fisher, *messages))
    received = [shifted(m, "wid", shift) for shift, m in enumerate(messages, 1)]
    high, low = split_fisher(fisher, *halves)
    own, high, low = lax.optimization_barrier((own, high, low))
    outer = outer_products(own, other, messages[0], received)
    gathered = [outer] + [exchanged(outer, steps) for steps in exchange_steps(seq_count)]
    parts = fisher_product(gathered, high, low, wid_count)
    result = parts[0]
    for shift in range(1, wid_count):
        result = result + shifted(parts[shift], "wid", shift)
    return result


def solution(mesh):
    placed = (
        P(("grp", "seq"), ("wid", "rep")),
        P(("grp", "seq"), ("wid", "rep")),
        P(("grp", "seq"), ("wid", "rep")),
        P(("grp", "seq"), ("wid", "rep")),
        P(("wid", "rep"), None, None),
        P(("wid", "rep")),
        P(("wid", "rep"), None, None),
        P(("wid", "rep")),
        P("seq", "wid"),
    )
    return jax.shard_map(
        shards,
        mesh=mesh,
        in_specs=placed,
        out_specs=P(("grp", "wid"), "rep", "seq"),
        check_vma=False,
    )
```

```python
import functools

import jax
import jax.numpy as jnp
from jax import lax
from jax.experimental import pallas as pl
from jax.experimental.pallas import tpu as pltpu
from jax.sharding import PartitionSpec as P

BLK = 128
LEN = 64
MXU = 256
PIECES = 8
NT = (((1,), (1,)), ((), ()))
F32 = jnp.float32
BF16 = jnp.bfloat16
VMEM = pl.BlockSpec(memory_space=pltpu.VMEM)
HBM = pl.BlockSpec(memory_space=pltpu.HBM)
PARAMS = pltpu.CompilerParams(vmem_limit_bytes=16 << 20)


def two_parts(x):
    high = x.astype(BF16)
    return high, (x - high.astype(F32)).astype(BF16)


def product(left, right, dims):
    left_high, left_low = two_parts(left)
    right_high, right_low = two_parts(right)
    dot = functools.partial(lax.dot_general, dimension_numbers=dims, preferred_element_type=F32)
    rows = left.shape[0]
    main = dot(jnp.concatenate([left_high, left_low], axis=0), right_high)
    return main[:rows] + (main[rows:] + dot(left_high, right_low))


def scaled_rows(rows, scale):
    return rows * jnp.concatenate([scale] * (rows.shape[0] // scale.shape[0]), axis=0)


def project_side(picked, scale_of, weights, side):
    _, chosen, pairs, _, _ = picked.shape
    tokens = jnp.concatenate(
        [
            jnp.concatenate(
                [scaled_rows(picked[side, block, pair], scale_of(block, pair)) for pair in range(pairs)],
                axis=0,
            )
            for block in range(chosen)
        ],
        axis=1,
    )
    factor = jnp.concatenate([weights[side, block] for block in range(chosen)], axis=1)
    return lax.dot_general(factor, tokens, NT, preferred_element_type=F32)


def project_other_kernel(
    act_index,
    grad_index,
    act_exponents,
    grad_exponents,
    act_blocks,
    grad_blocks,
    acts,
    grads,
    sent,
    picked_own,
    scales_own,
    weights,
    index,
    exponents,
    picked_other,
    small_sems,
    sems,
):
    own = lax.axis_index("rep")
    other = 1 - own
    _, chosen, pairs, _, _ = picked_own.shape
    block_count = exponents.shape[2]
    values = (acts, grads)
    small = []
    for place, (sources, target) in enumerate(
        (
            ((act_index, grad_index), index),
            ((act_exponents, grad_exponents), exponents),
            ((act_blocks, grad_blocks), weights),
        )
    ):
        for side, source in enumerate(sources):
            copy = pltpu.make_async_copy(source, target.at[side], small_sems.at[place, side])
            copy.start()
            small.append(copy)
    local = []
    for side in range(2):
        small[side].wait()
        local.append([lax.rem(index[side, block], block_count) for block in range(chosen)])
    copies = {}
    for place, (parity, target) in enumerate(((other, picked_other), (own, picked_own))):
        for side in range(2):
            for block in range(chosen):
                columns = pl.ds(pl.multiple_of(local[side][block] * BLK, BLK), BLK)
                copy = pltpu.make_async_copy(
                    values[side].at[:, parity, :, columns],
                    target.at[side, block],
                    sems.at[place, side, block],
                )
                copy.start()
                copies[place, side, block] = copy
    for copy in small[2:]:
        copy.wait()

    def scale_of(side, block, pair, parity):
        exponent = exponents[side, 2 * pair + parity, local[side][block]]
        return jnp.exp2(jnp.full((16, BLK), exponent, jnp.int32).astype(F32)).astype(BF16)

    for side in range(2):
        for block in range(chosen):
            for pair in range(pairs):
                scales_own[side, block, pair] = scale_of(side, block, pair, own)
    width = weights.shape[2]
    for side in range(2):
        for block in range(chosen):
            copies[0, side, block].wait()
        sent[side * width : (side + 1) * width, :] = project_side(
            picked_other, lambda block, pair: scale_of(side, block, pair, other), weights, side
        )
    for side in range(2):
        for block in range(chosen):
            copies[1, side, block].wait()


def project_other(indices, exponents, blocks, values):
    pairs, _, _, features = values[0].shape
    chosen, width, _ = blocks[0].shape
    tokens = pairs * LEN
    operands = [
        pltpu.with_memory_space_constraint(v, pltpu.HBM)
        for v in (*indices, *exponents, *blocks, *values)
    ]
    return pl.pallas_call(
        project_other_kernel,
        out_shape=(
            jax.ShapeDtypeStruct((2 * width, tokens), F32),
            jax.ShapeDtypeStruct((2, chosen, pairs, LEN, BLK), BF16),
            jax.ShapeDtypeStruct((2, chosen, pairs, 16, BLK), BF16),
            jax.ShapeDtypeStruct((2, chosen, width, BLK), BF16),
        ),
        in_specs=[HBM] * 8,
        out_specs=[VMEM] * 4,
        scratch_shapes=[
            pltpu.SMEM((2, chosen), jnp.int32),
            pltpu.SMEM((2, *exponents[0].shape), jnp.int32),
            pltpu.VMEM((2, chosen, pairs, LEN, BLK), BF16),
            pltpu.SemaphoreType.DMA((3, 2)),
            pltpu.SemaphoreType.DMA((2, 2, chosen)),
        ],
        cost_estimate=pl.CostEstimate(
            flops=4 * tokens * chosen * BLK * width,
            bytes_accessed=8 * tokens * chosen * BLK + 8 * tokens * width,
            transcendentals=0,
        ),
        compiler_params=PARAMS,
        name="project_other",
    )(*operands)


def project_own_kernel(picked, scales, weights, out):
    width = weights.shape[2]
    for side in range(2):
        out[side * width : (side + 1) * width, :] = project_side(
            picked, lambda block, pair: scales[side, block, pair], weights, side
        )


def project_own(picked, scales, weights):
    _, chosen, pairs, _, _ = picked.shape
    width = weights.shape[2]
    tokens = pairs * LEN
    return pl.pallas_call(
        project_own_kernel,
        out_shape=jax.ShapeDtypeStruct((2 * width, tokens), F32),
        in_specs=[VMEM] * 3,
        out_specs=VMEM,
        cost_estimate=pl.CostEstimate(
            flops=4 * tokens * chosen * BLK * width,
            bytes_accessed=4 * tokens * chosen * BLK + 8 * tokens * width,
            transcendentals=0,
        ),
        compiler_params=PARAMS,
        name="project_own",
    )(picked, scales, weights)


def split_pieces(fisher, high, low, held, sems):
    pieces, rows, _ = held.shape
    copies = [
        pltpu.make_async_copy(fisher.at[pl.ds(piece * rows, rows)], held.at[piece], sems.at[piece])
        for piece in range(pieces)
    ]
    for copy in copies:
        copy.start()
    for piece in range(pieces):
        copies[piece].wait()

        @pl.loop(0, rows // 16)
        def _(step):
            part_high, part_low = two_parts(held[piece, pl.ds(step * 16, 16), :])
            target = pl.ds(piece * rows + step * 16, 16)
            high[target, :] = part_high
            low[target, :] = part_low


def split_early_kernel(fisher, high, low, held, sems):
    @pl.when(lax.axis_index("rep") == 1)
    def _():
        split_pieces(fisher, high, low, held, sems)


def split_late_kernel(fisher, high_in, low_in, high, low, held, sems):
    first_core = lax.axis_index("rep") == 0

    @pl.when(first_core)
    def _():
        split_pieces(fisher, high, low, held, sems)

    @pl.when(~first_core)
    def _():
        @pl.loop(0, high.shape[0] // 16)
        def _(step):
            rows = pl.ds(pl.multiple_of(step * 16, 16), 16)
            high[rows, :] = high_in[rows, :]
            low[rows, :] = low_in[rows, :]


def split_fisher(fisher, *halves):
    rows, columns = fisher.shape
    half = jax.ShapeDtypeStruct((rows, columns), BF16)
    return pl.pallas_call(
        split_late_kernel if halves else split_early_kernel,
        out_shape=(half, half),
        in_specs=[HBM] + [VMEM] * len(halves),
        out_specs=(VMEM, VMEM),
        scratch_shapes=[
            pltpu.VMEM((PIECES, rows // PIECES, columns), F32),
            pltpu.SemaphoreType.DMA((PIECES,)),
        ],
        cost_estimate=pl.CostEstimate(
            flops=2 * rows * columns, bytes_accessed=8 * rows * columns, transcendentals=0
        ),
        compiler_params=PARAMS,
        name="split_late" if halves else "split_early",
    )(pltpu.with_memory_space_constraint(fisher, pltpu.HBM), *halves)


def message_kernel(width, own, other, *messages):
    wid = lax.axis_index("wid")
    count = len(messages) + 1
    share = width // count
    acts = own[:width, :] + other[:width, :]
    for shift, message in enumerate(messages, 1):
        target = lax.rem(wid + shift, count)
        rows = pl.ds(pl.multiple_of(width + target * share, share), share)
        message[:width, :] = acts
        message[width:, :] = own[rows, :] + other[rows, :]


def make_messages(own, other, wid_count):
    width = own.shape[0] // 2
    shape = jax.ShapeDtypeStruct((width + width // wid_count, own.shape[1]), F32)
    return pl.pallas_call(
        functools.partial(message_kernel, width),
        out_shape=[shape] * (wid_count - 1),
        in_specs=[VMEM] * 2,
        out_specs=[VMEM] * (wid_count - 1),
        compiler_params=PARAMS,
        name="make_messages",
    )(own, other)


def outer_kernel(width, own, other, *rest):
    *messages, out, staged = rest
    wid = lax.axis_index("wid")
    share = width // (len(messages) + 1)
    rows = pl.ds(pl.multiple_of(width + wid * share, share), share)
    acts = own[:width, :] + other[:width, :]
    grads = own[rows, :] + other[rows, :]
    for message in messages:
        acts = acts + message[:width, :]
        grads = grads + message[width:, :]
    half = share // 2
    pairs = acts.shape[1] // BLK
    lane = lax.broadcasted_iota(jnp.int32, (half, BLK), 1)
    for pair in range(pairs):
        staged[pair] = grads[:, pair * BLK : (pair + 1) * BLK]
    results = []
    for pair in range(pairs):
        pieces = []
        for odd in range(2):
            part = staged[pair, pl.ds(odd, half, stride=2), :]
            pieces.append(jnp.where(lane < LEN, part, 0.0))
            pieces.append(jnp.where(lane < LEN, 0.0, part))
        left = jnp.concatenate(pieces, axis=0)
        results.append(product(left, acts[:, pair * BLK : (pair + 1) * BLK], NT) * (1.0 / LEN))
    for pair, result in enumerate(results):
        both = jnp.concatenate([result[: 2 * half, :], result[2 * half :, :]], axis=1)
        out[pl.ds(2 * pair, half, stride=2 * pairs), :] = both[:half, :]
        out[pl.ds(2 * pair + 1, half, stride=2 * pairs), :] = both[half:, :]


def outer_products(own, other, messages):
    width = own.shape[0] // 2
    tokens = own.shape[1]
    share = width // (len(messages) + 1)
    sequences = tokens // LEN
    return pl.pallas_call(
        functools.partial(outer_kernel, width),
        out_shape=jax.ShapeDtypeStruct((share // 2 * sequences, 2 * width), F32),
        in_specs=[VMEM] * (2 + len(messages)),
        out_specs=VMEM,
        scratch_shapes=[pltpu.VMEM((tokens // BLK, share, BLK), F32)],
        compiler_params=PARAMS,
        name="outer_products",
    )(own, other, *messages)


def tile_products(left_high, left_low, high, low):
    rows, columns = high.shape
    streamed = rows // 4 // MXU * MXU
    middle = streamed + MXU if streamed else rows // 2
    count = left_high.shape[0]
    both = jnp.concatenate([left_high, left_low], axis=0)
    dot = functools.partial(lax.dot_general, dimension_numbers=NT, preferred_element_type=F32)
    sums = None
    for start in range(0, columns, MXU):
        piece = slice(start, start + MXU)
        terms = []
        terms.append(dot(both[:, piece], high[streamed:middle, piece]))
        if streamed:
            terms.append(dot(high[:streamed, piece], both[:, piece]))
        terms.append(dot(both[:, piece], high[middle:, piece]))
        if streamed:
            terms.append(dot(low[:streamed, piece], left_high[:, piece]))
        terms.append(dot(left_high[:, piece], low[streamed:middle, piece]))
        terms.append(dot(left_high[:, piece], low[middle:, piece]))
        sums = terms if sums is None else [a + b for a, b in zip(sums, terms)]
    tall_high, tall_low = (sums.pop(1), sums.pop(2)) if streamed else (None, None)
    held_high = jnp.concatenate(sums[:2], axis=1)
    held_low = jnp.concatenate(sums[2:], axis=1)
    result = held_high[:count] + (held_high[count:] + held_low)
    if streamed:
        tall = tall_high[:, :count] + (tall_high[:, count:] + tall_low)
        result = jnp.concatenate([tall.T, result], axis=1)
    return result


def exchange_steps(seq_count):
    steps = range(1, seq_count)
    return list(zip(steps, sorted(steps, key=lambda step: (step.bit_count(), -step))))


def fisher_kernel(*refs):
    seq_count = len(refs) - 3
    wid_count, owned = refs[-1].shape[:2]
    gathered = refs[:seq_count]
    high, low = refs[seq_count : seq_count + 2]
    out = refs[-1]
    seq = lax.axis_index("seq")
    wid = lax.axis_index("wid")
    per_wid = seq_count // wid_count
    sequences = owned // per_wid
    steps = gathered[0].shape[0] // sequences
    rows = []
    for ref in gathered:
        rows.append(
            jnp.concatenate(
                [ref[step * sequences : (step + 1) * sequences, :] for step in range(steps)], axis=1
            )
        )
    left_high, left_low = two_parts(jnp.concatenate(rows, axis=0))
    result = tile_products(left_high, left_low, high, low)
    rep = lax.axis_index("rep")
    for shift, (first, second) in enumerate([(0, 0)] + exchange_steps(seq_count)):
        group = seq ^ jnp.where(rep == 0, first, second)
        target = lax.rem(group // per_wid - wid + wid_count, wid_count)
        rows = pl.ds(pl.multiple_of(lax.rem(group, per_wid) * sequences, sequences), sequences)
        out[target, rows, 0, :] = result[shift * sequences : (shift + 1) * sequences]


def fisher_product(gathered, high, low, wid_count):
    seq_count = len(gathered)
    rows, columns = high.shape
    sequences = gathered[0].shape[0] * BLK // columns
    per_wid = seq_count // wid_count
    return pl.pallas_call(
        fisher_kernel,
        out_shape=jax.ShapeDtypeStruct((wid_count, per_wid * sequences, 1, rows), F32),
        in_specs=[VMEM] * (seq_count + 2),
        out_specs=VMEM,
        compiler_params=PARAMS,
        name="fisher_product",
    )(*gathered, high, low)


def shifted(value, axis, shift):
    count = lax.axis_size(axis)
    return lax.ppermute(value, axis, [(i, (i + shift) % count) for i in range(count)])


def exchanged(value, steps):
    cores = lax.axis_size("rep")
    pairs = [
        (seq * cores + core, (seq ^ steps[core]) * cores + core)
        for seq in range(lax.axis_size("seq"))
        for core in range(cores)
    ]
    return lax.ppermute(value, ("seq", "rep"), pairs)


def shards(
    activations,
    output_grads,
    act_exponents,
    grad_exponents,
    input_blocks,
    input_index,
    output_blocks,
    output_index,
    fisher_inverse,
):
    seq_count = lax.axis_size("seq")
    wid_count = lax.axis_size("wid")
    pairs = activations.shape[0] // LEN // 2
    indices = (input_index, output_index)
    exponents = (act_exponents, grad_exponents)
    blocks = (jnp.swapaxes(input_blocks, 1, 2), jnp.swapaxes(output_blocks, 1, 2))
    values = tuple(v.reshape(pairs, 2, LEN, v.shape[1]) for v in (activations, output_grads))
    sent, *held = project_other(indices, exponents, blocks, values)
    other = shifted(sent, "rep", 1)
    own = project_own(*held)
    fisher, own = lax.optimization_barrier((fisher_inverse, own))
    halves = split_fisher(fisher)
    own, other, *halves = lax.optimization_barrier((own, other, *halves))
    messages = make_messages(own, other, wid_count)
    fisher, *messages = lax.optimization_barrier((fisher, *messages))
    received = [shifted(m, "wid", shift) for shift, m in enumerate(messages, 1)]
    high, low = split_fisher(fisher, *halves)
    own, high, low = lax.optimization_barrier((own, high, low))
    outer = outer_products(own, other, received)
    gathered = [outer] + [exchanged(outer, steps) for steps in exchange_steps(seq_count)]
    parts = fisher_product(gathered, high, low, wid_count)
    result = parts[0]
    for shift in range(1, wid_count):
        result = result + shifted(parts[shift], "wid", shift)
    return result


def solution(mesh):
    placed = (
        P(("grp", "seq"), ("wid", "rep")),
        P(("grp", "seq"), ("wid", "rep")),
        P(("grp", "seq"), ("wid", "rep")),
        P(("grp", "seq"), ("wid", "rep")),
        P(("wid", "rep"), None, None),
        P(("wid", "rep")),
        P(("wid", "rep"), None, None),
        P(("wid", "rep")),
        P("seq", "wid"),
    )
    return jax.shard_map(
        shards,
        mesh=mesh,
        in_specs=placed,
        out_specs=P(("grp", "wid"), "rep", "seq"),
        check_vma=False,
    )
```
